256 devices in a mesh: freq: 64 (over y, z, x_hi), tm: 4 (over x_lo, core).
Axes of the slice: x: 4 (x_hi: 2, x_lo: 2; x = x_hi * 2 + x_lo), y: 4, z: 8, core: 2. Of those that a mesh axis runs over, the one named last changes fastest.
Arguments:
- voltages: int32 [1024, 32, 2, 4096], P('freq', 'tm'), may hold values from -127 to 127
- tile_map: int32 [36], replicated, may hold values from 0 to 35, each once
Outputs:
- visibilities: float32 [36, 128, 2, 128, 128], P('tm', 'freq')
The draws below stay inside these ranges and needn't reach their ends.
Inputs may be any that keep to these rules, and one draw needn't show every extreme that they name: `tile_map`: a permutation of the tile ids.
All inputs are finite; a program needn't handle non-finite values.
Results may differ from the reference program's by a relative error of at most 0.0052.
Values may be sent and summed in bfloat16 or wider, within the bound.
A program may use at most 128 MiB of HBM per device.

```python
import math
import jax
import jax.numpy as jnp
from jax import lax

NCHAN = 4096
TAPS = 4
TB = 128
N_IN = 1024
SPECTRA = 32
CHANNELS = 128
FIRST = 1984
NTILES = 36


def touch_ends(array, rng, least, largest):
    place = [jax.random.randint(jax.random.fold_in(rng, axis), (), 0, length) for axis, length in enumerate(array.shape)]
    widest = array.shape.index(max(array.shape))
    beside = place[:widest] + [(place[widest] + 1) % array.shape[widest]] + place[widest + 1:]
    return array.at[tuple(place)].set(least).at[tuple(beside)].set(largest)


def setup_inputs(seed: int = 0) -> dict:
    splits = jax.random.split(jax.random.key(seed), 3)
    voltages = touch_ends(jax.random.randint(splits[0], (N_IN, SPECTRA, 2, NCHAN), -127, 128), jax.random.fold_in(splits[0], 1), -127, 127).astype(jnp.int32)
    tile_map = jax.random.permutation(splits[1], NTILES).astype(jnp.int32)
    return {"voltages": voltages, "tile_map": tile_map}


def filter_table(channels, first_channel):
    sample_idx = jnp.arange(TAPS * NCHAN, dtype=jnp.int32)
    position = (sample_idx.astype(jnp.float32) + 0.5) / NCHAN - TAPS / 2.0
    hann_taper = 0.5 - 0.5 * jnp.cos((sample_idx.astype(jnp.float32) + 0.5) * (2.0 * math.pi / (TAPS * NCHAN)))
    prototype = (jnp.sinc(position) * hann_taper / (128.0 * math.sqrt(NCHAN))).reshape(TAPS, NCHAN)
    sample_col = jnp.arange(NCHAN, dtype=jnp.int32)
    channel_row = first_channel + jnp.arange(channels, dtype=jnp.int32)
    phase_index = sample_col[:, None] * channel_row[None, :] % NCHAN
    angles = phase_index.astype(jnp.float32) * (2.0 * math.pi / NCHAN)
    cosine = jnp.cos(angles)
    sine_part = jnp.sin(angles)
    upper = jnp.stack([cosine, -sine_part], axis=-1)
    lower = jnp.stack([sine_part, cosine], axis=-1)
    pattern = jnp.stack([upper, lower], axis=0)
    table = prototype[:, None, :, None, None] * pattern[None]
    return table.astype(jnp.bfloat16).reshape(TAPS, 2 * NCHAN, 2 * channels)

def tile_coords(tile_id, blocks):
    step_row = jnp.arange(1, blocks, dtype=jnp.int32)
    triangle = step_row * (step_row + 1) // 2
    row_block = lax.optimization_barrier(jnp.sum((tile_id[..., None] >= triangle).astype(jnp.int32), axis=-1))
    col_block = tile_id - row_block * (row_block + 1) // 2
    return (row_block.astype(jnp.int32), col_block.astype(jnp.int32))

def reference(voltages, tile_map):
    filters = filter_table(CHANNELS, FIRST)
    grouped = voltages.reshape(N_IN // 16, 16, SPECTRA, 2 * NCHAN)

    def channelize(input_group):
        samples = input_group.astype(jnp.bfloat16)
        extended = jnp.concatenate([jnp.zeros((16, TAPS - 1, 2 * NCHAN), jnp.bfloat16), samples], axis=1)
        accum_sum = jnp.zeros((16 * SPECTRA, 2 * CHANNELS), jnp.float32)
        for tap_index in range(TAPS):
            window = extended[:, tap_index:tap_index + SPECTRA].reshape(16 * SPECTRA, 2 * NCHAN)
            accum_sum = accum_sum + jnp.dot(window, filters[tap_index], preferred_element_type=jnp.float32)
        return accum_sum.astype(jnp.bfloat16)
    spectra = lax.map(channelize, grouped)
    spectra = spectra.reshape(N_IN, SPECTRA, CHANNELS, 2).transpose(2, 3, 1, 0)

    def one_tile(tile_id):
        row_block, col_block = tile_coords(tile_id, N_IN // TB)
        row_tiles = lax.dynamic_slice_in_dim(spectra, row_block * TB, TB, 3).astype(jnp.float32)
        col_tiles = lax.dynamic_slice_in_dim(spectra, col_block * TB, TB, 3).astype(jnp.float32)
        turned = jnp.stack([row_tiles[:, 1], -row_tiles[:, 0]], axis=1)
        paired = jnp.stack([row_tiles, turned], axis=1)
        products = jnp.einsum('hqptx,hpty->hqxy', paired, col_tiles, precision=lax.Precision.HIGHEST)
        return products * (1.0 / SPECTRA)
    return lax.map(one_tile, tile_map)
```

```python
import functools
import math

import jax
import jax.numpy as jnp
import numpy as np
from jax import lax
from jax.experimental import pallas as pl
from jax.experimental.pallas import tpu as pltpu
from jax.sharding import PartitionSpec as P

NCHAN = 4096
TAPS = 4
TB = 128
CHANNELS = 128
FIRST = NCHAN // 2 - CHANNELS // 2
CH_DEV = 2
LANES = 128
CHUNKS = NCHAN // LANES
ROWS = 2 * CHUNKS
HALF = ROWS // 2
BLOCKS = 8
OUT = BLOCKS + TAPS - 1
PATHS = 16
SLOT = 16
SPECTRA = 32
QUADS = CHANNELS // 4
MESH = pl.DeviceIdType.MESH


def window_table():
    n = np.arange(TAPS * NCHAN, dtype=np.float64) + 0.5
    taper = 0.5 - 0.5 * np.cos(2.0 * math.pi * n / (TAPS * NCHAN))
    taps = np.sinc(n / NCHAN - TAPS / 2.0) * taper / (128.0 * math.sqrt(NCHAN))
    taps = np.repeat(taps.reshape(TAPS, CHUNKS, 1, LANES), 2, axis=2)
    return taps.reshape(TAPS, ROWS, LANES).astype(np.float32)


def turn_table():
    sample = np.arange(LANES)[:, None]
    m = np.arange(CHANNELS)[None, :]
    angle = (sample * (FIRST + m) % NCHAN) * (2.0 * math.pi / NCHAN)
    first = np.concatenate([np.cos(angle), -np.sin(angle)], axis=1)
    sign = np.tile(1.0 - 2.0 * (m % 2), (1, 2))
    table = np.concatenate([first, first * sign], axis=0).astype(np.float32)
    high = table.astype(jnp.bfloat16)
    low = (table - high.astype(np.float32)).astype(jnp.bfloat16)
    return np.concatenate([high, low], axis=0)


def run_table():
    run = np.arange(HALF)[:, None] // 2
    part = np.arange(HALF)[:, None] % 2
    m = np.arange(CHANNELS)[None, :]
    angle = (run * LANES * (FIRST + m) % NCHAN) * (2.0 * math.pi / NCHAN)
    turned = np.exp(-1j * angle) * np.where(part == 0, 1.0, 1j)
    return np.stack([turned.real, turned.imag]).astype(np.float32)


def quad_table():
    table = np.arange(QUADS)[:, None] == np.arange(CHANNELS)[None, :] // 4
    return table.astype(jnp.bfloat16)


def place_table(times):
    table = np.zeros((times, 2, 2, 2, SLOT, 2, 2, 2, SPECTRA), np.float32)
    for t in range(times):
        for step in range(OUT):
            if t * BLOCKS + step < times * BLOCKS:
                for e in range(2):
                    for c in range(2):
                        for q in range(2):
                            table[t, e, c, q, step, e, c, q, t * BLOCKS + step] = 1.0
    return table.reshape(times * LANES, 2 * LANES).astype(jnp.bfloat16)


def front(
    freqs,
    times,
    x_hbm,
    window,
    turn,
    runs,
    quads,
    place,
    spectra,
    x,
    z,
    sums,
    mixed,
    packed,
    landed,
    ready,
    x_sem,
    slice_send,
    slice_recv,
    own_sem,
    spread_send,
    spread_recv,
):
    f, t = lax.axis_index("freq"), lax.axis_index("tm")
    group = freqs // times
    rows = group // 2 * PATHS
    among = (f // group == t).astype(jnp.int32)
    per_path = BLOCKS * ROWS

    def fetch(i):
        at = pl.ds(pl.multiple_of(i * per_path, per_path), per_path)
        return pltpu.make_async_copy(x_hbm.at[at], x.at[at], x_sem.at[i])

    def start_fetch(i, carry):
        fetch(i).start()
        return carry

    lax.fori_loop(0, PATHS, start_fetch, 0)

    barrier = pltpu.get_barrier_semaphore()
    for d in range(1, times):
        pl.semaphore_signal(
            barrier, inc=1, device_id=(f, lax.rem(t + d, times)), device_id_type=MESH
        )

    def greet(j, carry):
        @pl.when((j != f) | (among == 0))
        def _():
            pl.semaphore_signal(
                barrier, inc=1, device_id=(j, f // group), device_id_type=MESH
            )

        return carry

    lax.fori_loop(0, freqs, greet, 0)
    sums[...] = jnp.zeros_like(sums)

    def channelize(i, carry):
        fetch(i).wait()
        for g in range(ROWS // 16):
            taps = [window[k, g * 16 : (g + 1) * 16, :] for k in range(TAPS)]
            steps = []
            for b in range(BLOCKS):
                at = pl.multiple_of(i * per_path + b * ROWS + g * 16, 16)
                steps.append(x[pl.ds(at, 16), :].astype(jnp.float32))
            for s in range(OUT):
                terms = [
                    taps[k] * steps[s - TAPS + 1 + k]
                    for k in range(TAPS)
                    if 0 <= s - TAPS + 1 + k < BLOCKS
                ]
                total = functools.reduce(lambda a, b: a + b, terms)
                at, side = s * HALF + g % 2 * 16, g // 2 * LANES
                z[at : at + 16, side : side + LANES] = total.astype(jnp.bfloat16)
        value = z[...]
        u = jnp.dot(
            jnp.concatenate([value, value], axis=1),
            turn[...],
            preferred_element_type=jnp.float32,
        )
        real, imag = runs[0], runs[1]
        at = pl.multiple_of(i * 2 * SLOT, 2 * SLOT)
        for s in range(OUT):
            u0 = u[s * HALF : (s + 1) * HALF, :LANES]
            u1 = u[s * HALF : (s + 1) * HALF, LANES:]
            a = jnp.sum(real * u0 - imag * u1, axis=0, keepdims=True)
            b = jnp.sum(imag * u0 + real * u1, axis=0, keepdims=True)
            sums[pl.ds(at + s, 1), :] = a
            sums[pl.ds(at + SLOT + s, 1), :] = b
        return carry

    lax.fori_loop(0, PATHS, channelize, 0)

    of_quad = lax.broadcasted_iota(jnp.int32, (2 * SLOT, LANES), 1) % 4
    for i in range(PATHS):
        value = sums[i * 2 * SLOT : (i + 1) * 2 * SLOT, :]
        four = jnp.concatenate(
            [jnp.where(of_quad == m, value, 0.0) for m in range(4)], axis=0
        ).astype(jnp.bfloat16)
        moved = lax.dot_general(
            quads[...],
            four,
            (((1,), (1,)), ((), ())),
            preferred_element_type=jnp.float32,
        )
        mixed[pl.ds(i, QUADS, stride=PATHS), :] = moved
    packed[...] = mixed[...].astype(jnp.bfloat16)

    pl.semaphore_wait(barrier, times - 1 + freqs - among)
    slices = []
    for d in range(1, times):
        to = lax.rem(t + d, times)
        copy = pltpu.make_async_remote_copy(
            src_ref=packed.at[pl.ds(pl.multiple_of(to * rows, rows), rows)],
            dst_ref=landed.at[t],
            send_sem=slice_send.at[d - 1],
            recv_sem=slice_recv.at[d - 1],
            device_id=(f, to),
            device_id_type=MESH,
        )
        copy.start()
        slices.append(copy)
    landed[t] = packed[pl.ds(pl.multiple_of(t * rows, rows), rows), :]
    for copy in slices:
        copy.wait_recv()

    joined = jnp.dot(
        jnp.concatenate([landed[j] for j in range(times)], axis=1),
        place[...],
        preferred_element_type=jnp.float32,
    ).astype(jnp.bfloat16)
    for e in range(2):
        ready[e] = joined[:, e * LANES : (e + 1) * LANES]

    here = spectra.at[pl.ds(pl.multiple_of(f * PATHS, PATHS), PATHS)]

    def spread(j, carry):
        k = lax.rem(j + f, freqs)
        number, time = k // times, lax.rem(k, times)
        at = pl.ds(pl.multiple_of(number // 2 * PATHS, PATHS), PATHS)
        tile = ready.at[lax.rem(number, 2), at]
        to = t * group + number
        local = (to == f) & (time == t)

        @pl.when(local)
        def _():
            pltpu.make_async_copy(tile, here, own_sem).start()

        @pl.when(jnp.logical_not(local))
        def _():
            pltpu.make_async_remote_copy(
                src_ref=tile,
                dst_ref=here,
                send_sem=spread_send,
                recv_sem=spread_recv,
                device_id=(to, time),
                device_id_type=MESH,
            ).start()

        return carry

    lax.fori_loop(0, freqs, spread, 0)
    for copy in slices:
        copy.wait_send()

    def drain(count):
        some = spectra.at[pl.ds(0, count * PATHS)]
        pltpu.make_async_copy(some, some, spread_send).wait()
        pltpu.make_async_copy(some, some, spread_recv).wait()

    @pl.when(among == 1)
    def _():
        tile = ready.at[0, pl.ds(0, PATHS)]
        pltpu.make_async_copy(tile, here, own_sem).wait()
        drain(freqs - 1)

    @pl.when(among == 0)
    def _():
        drain(freqs)


def correlate(slots, ids, spectra, out, tiles, sems):
    t = lax.axis_index("tm")
    lane = lax.broadcasted_iota(jnp.int32, (TB, LANES), 1)
    first = lane < LANES // 2
    even = lane // SPECTRA % 2 == 0
    for j in range(slots):
        number = ids[t * slots + j]
        row = jnp.int32(0)
        for k in range(1, 8):
            row = row + (number >= k * (k + 1) // 2).astype(jnp.int32)
        col = number - row * (row + 1) // 2
        left = spectra[pl.ds(pl.multiple_of(row * TB, TB), TB), :].astype(jnp.float32)
        right = spectra[pl.ds(pl.multiple_of(col * TB, TB), TB), :]
        turned = jnp.where(
            even,
            pltpu.roll(left, LANES - SPECTRA, 1),
            -pltpu.roll(left, SPECTRA, 1),
        )
        four = jnp.concatenate(
            [
                jnp.where(first, left, 0.0),
                jnp.where(first, turned, 0.0),
                jnp.where(first, 0.0, left),
                jnp.where(first, 0.0, turned),
            ],
            axis=0,
        ).astype(jnp.bfloat16)
        products = lax.dot_general(
            four, right, (((1,), (1,)), ((), ())), preferred_element_type=jnp.float32
        )
        tiles[j] = (products * (1.0 / SPECTRA)).reshape(CH_DEV, 2, TB, TB)
        pltpu.make_async_copy(tiles.at[j], out.at[j], sems.at[j]).start()
    for j in range(slots):
        pltpu.make_async_copy(tiles.at[j], out.at[j], sems.at[j]).wait()


def run_front(freqs, times, samples):
    rows = freqs // times // 2 * PATHS
    dma = pltpu.SemaphoreType.DMA
    vmem = pl.BlockSpec(memory_space=pltpu.VMEM)
    return pl.pallas_call(
        functools.partial(front, freqs, times),
        out_shape=jax.ShapeDtypeStruct((freqs * PATHS, LANES), jnp.bfloat16),
        in_specs=[pl.BlockSpec(memory_space=pltpu.HBM)] + [vmem] * 5,
        out_specs=pl.BlockSpec(memory_space=pl.ANY),
        scratch_shapes=[
            pltpu.VMEM((PATHS * BLOCKS * ROWS, LANES), jnp.int32),
            pltpu.VMEM((OUT * HALF, 2 * LANES), jnp.bfloat16),
            pltpu.VMEM((PATHS * 2 * SLOT, LANES), jnp.float32),
            pltpu.VMEM((QUADS * PATHS, LANES), jnp.float32),
            pltpu.VMEM((QUADS * PATHS, LANES), jnp.bfloat16),
            pltpu.VMEM((times, rows, LANES), jnp.bfloat16),
            pltpu.VMEM((2, rows, LANES), jnp.bfloat16),
            dma((PATHS,)),
            dma((times - 1,)),
            dma((times - 1,)),
            dma,
            dma,
            dma,
        ],
        compiler_params=pltpu.CompilerParams(
            collective_id=0, has_side_effects=True, vmem_limit_bytes=60 * 2**20
        ),
        name="front",
    )(
        samples,
        jnp.asarray(window_table()),
        jnp.asarray(turn_table()),
        jnp.asarray(run_table()),
        jnp.asarray(quad_table()),
        jnp.asarray(place_table(times)),
    )


def run_correlate(slots, tile_map, spectra):
    return pl.pallas_call(
        functools.partial(correlate, slots),
        out_shape=jax.ShapeDtypeStruct((slots, CH_DEV, 2, TB, TB), jnp.float32),
        in_specs=[
            pl.BlockSpec(memory_space=pltpu.SMEM),
            pl.BlockSpec(memory_space=pltpu.VMEM),
        ],
        out_specs=pl.BlockSpec(memory_space=pl.ANY),
        scratch_shapes=[
            pltpu.VMEM((slots, CH_DEV, 2, TB, TB), jnp.float32),
            pltpu.SemaphoreType.DMA((slots,)),
        ],
        compiler_params=pltpu.CompilerParams(vmem_limit_bytes=40 * 2**20),
        name="correlate",
    )(tile_map, spectra)


def on_device(voltages, tile_map):
    freqs, times = lax.axis_size("freq"), lax.axis_size("tm")
    samples = voltages.reshape(PATHS, BLOCKS, 2, CHUNKS, LANES)
    samples = samples.transpose(0, 1, 3, 2, 4).reshape(PATHS * BLOCKS * ROWS, LANES)
    spectra = run_front(freqs, times, samples)
    return run_correlate(tile_map.shape[0] // times, tile_map, spectra)


def solution(mesh):
    in_specs = (P("freq", "tm", None, None), P())
    out_specs = P("tm", "freq", None, None, None)
    return jax.shard_map(
        on_device, mesh=mesh, in_specs=in_specs, out_specs=out_specs, check_vma=False
    )
```

```python
import functools
import math

import jax
import jax.numpy as jnp
import numpy as np
from jax import lax
from jax.experimental import pallas as pl
from jax.experimental.pallas import tpu as pltpu
from jax.sharding import PartitionSpec as P

NCHAN = 4096
TAPS = 4
TB = 128
CHANNELS = 128
FIRST = NCHAN // 2 - CHANNELS // 2
CH_DEV = 2
LANES = 128
CHUNKS = NCHAN // LANES
ROWS = 2 * CHUNKS
HALF = ROWS // 2
BLOCKS = 8
OUT = BLOCKS + TAPS - 1
PATHS = 16
SLOT = 16
SPECTRA = 32
QUADS = CHANNELS // 4
BATCH = 4
PARTS = 4
MESH = pl.DeviceIdType.MESH


def window_table():
    n = np.arange(TAPS * NCHAN, dtype=np.float64) + 0.5
    taper = 0.5 - 0.5 * np.cos(2.0 * math.pi * n / (TAPS * NCHAN))
    taps = np.sinc(n / NCHAN - TAPS / 2.0) * taper / (128.0 * math.sqrt(NCHAN))
    taps = np.repeat(taps.reshape(TAPS, CHUNKS, 1, LANES), 2, axis=2)
    return taps.reshape(TAPS, ROWS, LANES).astype(np.float32)


def turn_table():
    sample = np.arange(LANES)[:, None]
    m = np.arange(CHANNELS)[None, :]
    angle = (sample * (FIRST + m) % NCHAN) * (2.0 * math.pi / NCHAN)
    first = np.concatenate([np.cos(angle), -np.sin(angle)], axis=1)
    sign = np.tile(1.0 - 2.0 * (m % 2), (1, 2))
    table = np.concatenate([first, first * sign], axis=0).astype(np.float32)
    high = table.astype(jnp.bfloat16)
    low = (table - high.astype(np.float32)).astype(jnp.bfloat16)
    return np.concatenate([high, low], axis=0)


def run_table():
    run = np.arange(HALF)[:, None] // 2
    part = np.arange(HALF)[:, None] % 2
    m = np.arange(CHANNELS)[None, :]
    angle = (run * LANES * (FIRST + m) % NCHAN) * (2.0 * math.pi / NCHAN)
    turned = np.exp(-1j * angle) * np.where(part == 0, 1.0, 1j)
    return np.stack([turned.real, turned.imag]).astype(np.float32)


def quad_table():
    table = np.arange(QUADS)[:, None] == np.arange(CHANNELS)[None, :] // 4
    return table.astype(jnp.bfloat16)


def place_table(times):
    table = np.zeros((times, 2, 2, 2, SLOT, 2, 2, 2, SPECTRA), np.float32)
    for t in range(times):
        for step in range(OUT):
            if t * BLOCKS + step < times * BLOCKS:
                for e in range(2):
                    for c in range(2):
                        for q in range(2):
                            table[t, e, c, q, step, e, c, q, t * BLOCKS + step] = 1.0
    return table.reshape(times * LANES, 2 * LANES).astype(jnp.bfloat16)


def front(
    freqs,
    times,
    x_hbm,
    window_hbm,
    turn_hbm,
    runs_hbm,
    quads_hbm,
    place_hbm,
    spectra,
    x,
    window,
    turn,
    runs,
    quads,
    place,
    z,
    sums,
    mixed,
    packed,
    landed,
    ready,
    x_sem,
    table_sem,
    slice_send,
    slice_recv,
    spread_send,
    spread_recv,
    share_send,
    share_recv,
):
    f, t = lax.axis_index("freq"), lax.axis_index("tm")
    group = freqs // times
    rows = group // 2 * PATHS
    half = freqs // 2
    core, mine = f // half, lax.rem(t, 2)
    among = ((f // group == t) & (core == mine)).astype(jnp.int32)
    per_path = BLOCKS * ROWS

    def fetch(i):
        at = pl.ds(pl.multiple_of(i * per_path, per_path), per_path)
        return pltpu.make_async_copy(x_hbm.at[at], x.at[at], x_sem.at[i])

    def start_fetch(i, carry):
        fetch(i).start()
        return carry

    tables = [
        pltpu.make_async_copy(source, target, table_sem.at[k])
        for k, (source, target) in enumerate(
            zip(
                (window_hbm, turn_hbm, runs_hbm, quads_hbm, place_hbm),
                (window, turn, runs, quads, place),
            )
        )
    ]
    tables[0].start()
    lax.fori_loop(0, BATCH, start_fetch, 0)
    for table in tables[1:]:
        table.start()
    lax.fori_loop(BATCH, PATHS, start_fetch, 0)

    barrier = pltpu.get_barrier_semaphore()
    for d in range(1, times):
        pl.semaphore_signal(
            barrier, inc=1, device_id=(f, lax.rem(t + d, times)), device_id_type=MESH
        )

    def greet(j, carry):
        source = half * mine + j

        @pl.when((source != f) | (f // group != t))
        def _():
            pl.semaphore_signal(
                barrier, inc=1, device_id=(source, f // group), device_id_type=MESH
            )

        return carry

    lax.fori_loop(0, half, greet, 0)
    sums[...] = jnp.zeros_like(sums)

    tables[0].wait()

    def channelize(n, carry):
        def filtered(j, carry):
            path, pair = j // 2, lax.rem(j, 2) * 16

            @pl.when(pair == 0)
            def _():
                fetch(n * BATCH + path).wait()

            for h in range(2):
                rows_at = h * HALF + pair
                start = (n * BATCH + path) * per_path + rows_at
                taps = [
                    window[k, pl.ds(pl.multiple_of(rows_at, 16), 16), :]
                    for k in range(TAPS)
                ]
                steps = [
                    x[pl.ds(pl.multiple_of(start + b * ROWS, 16), 16), :].astype(
                        jnp.float32
                    )
                    for b in range(BLOCKS)
                ]
                for s in range(OUT):
                    terms = [
                        taps[k] * steps[s - TAPS + 1 + k]
                        for k in range(TAPS)
                        if 0 <= s - TAPS + 1 + k < BLOCKS
                    ]
                    total = functools.reduce(lambda a, b: a + b, terms)
                    at = pl.multiple_of((path * OUT + s) * HALF + pair, 16)
                    z[pl.ds(at, 16), h * LANES : (h + 1) * LANES] = total.astype(
                        jnp.bfloat16
                    )
            return carry

        lax.fori_loop(0, 2 * BATCH, filtered, 0)

        @pl.when(n == 0)
        def _():
            tables[1].wait()
            tables[2].wait()

        value = z[...]
        u = jnp.dot(
            jnp.concatenate([value, value], axis=1),
            turn[...],
            preferred_element_type=jnp.float32,
        )
        real, imag = runs[0], runs[1]
        for path in range(BATCH):
            at = pl.multiple_of((n * BATCH + path) * 2 * SLOT, 2 * SLOT)
            for s in range(OUT):
                k = (path * OUT + s) * HALF
                u0, u1 = u[k : k + HALF, :LANES], u[k : k + HALF, LANES:]
                a = jnp.sum(real * u0 - imag * u1, axis=0, keepdims=True)
                b = jnp.sum(imag * u0 + real * u1, axis=0, keepdims=True)
                sums[pl.ds(at + s, 1), :] = a
                sums[pl.ds(at + SLOT + s, 1), :] = b
        return carry

    lax.fori_loop(0, PATHS // BATCH, channelize, 0)
    tables[3].wait()
    tables[4].wait()

    of_quad = lax.broadcasted_iota(jnp.int32, (2 * SLOT, LANES), 1) % 4
    for i in range(PATHS):
        value = sums[i * 2 * SLOT : (i + 1) * 2 * SLOT, :]
        four = jnp.concatenate(
            [jnp.where(of_quad == m, value, 0.0) for m in range(4)], axis=0
        ).astype(jnp.bfloat16)
        moved = lax.dot_general(
            quads[...],
            four,
            (((1,), (1,)), ((), ())),
            preferred_element_type=jnp.float32,
        )
        mixed[pl.ds(i, QUADS, stride=PATHS), :] = moved
    packed[...] = mixed[...].astype(jnp.bfloat16)

    pl.semaphore_wait(barrier, times - 1 + 2 * group - among)
    slices = []
    for d in range(1, times):
        to = lax.rem(t + d, times)
        copy = pltpu.make_async_remote_copy(
            src_ref=packed.at[pl.ds(pl.multiple_of(to * rows, rows), rows)],
            dst_ref=landed.at[t],
            send_sem=slice_send.at[d - 1],
            recv_sem=slice_recv.at[d - 1],
            device_id=(f, to),
            device_id_type=MESH,
        )
        copy.start()
        slices.append(copy)
    landed[t] = packed[pl.ds(pl.multiple_of(t * rows, rows), rows), :]
    for copy in slices:
        copy.wait_recv()

    joined = jnp.dot(
        jnp.concatenate([landed[j] for j in range(times)], axis=1),
        place[...],
        preferred_element_type=jnp.float32,
    ).astype(jnp.bfloat16)
    for e in range(2):
        ready[e] = joined[:, e * LANES : (e + 1) * LANES]

    here = spectra.at[pl.ds(pl.multiple_of(f * PATHS, PATHS), PATHS)]
    part = half // PARTS
    arrived = spread_recv.at[lax.rem(f // part, PARTS)]

    def spread(j, carry):
        k = lax.rem(j + f, 2 * group)
        number, time = k // 2, 2 * lax.rem(k, 2) + core
        at = pl.ds(pl.multiple_of(number // 2 * PATHS, PATHS), PATHS)
        tile = ready.at[lax.rem(number, 2), at]
        to = t * group + number
        local = (to == f) & (time == t)

        @pl.when(local)
        def _():
            pltpu.make_async_copy(tile, here, arrived).start()

        @pl.when(jnp.logical_not(local))
        def _():
            pltpu.make_async_remote_copy(
                src_ref=tile,
                dst_ref=here,
                send_sem=spread_send,
                recv_sem=arrived,
                device_id=(to, time),
                device_id_type=MESH,
            ).start()

        return carry

    lax.fori_loop(0, 2 * group, spread, 0)

    mate = t + 1 - 2 * mine
    shared = []
    for k in range(PARTS):
        at = (mine * PARTS + k) * part * PATHS
        some = spectra.at[pl.ds(pl.multiple_of(at, part * PATHS), part * PATHS)]
        pltpu.make_async_copy(some, some, spread_recv.at[k]).wait()
        copy = pltpu.make_async_remote_copy(
            src_ref=some,
            dst_ref=some,
            send_sem=share_send.at[k],
            recv_sem=share_recv.at[k],
            device_id=(f, mate),
            device_id_type=MESH,
        )
        copy.start()
        shared.append(copy)
    for copy in slices:
        copy.wait_send()

    def drain(count):
        some = spectra.at[pl.ds(0, count * PATHS)]
        pltpu.make_async_copy(some, some, spread_send).wait()

    @pl.when(among == 1)
    def _():
        drain(2 * group - 1)

    @pl.when(among == 0)
    def _():
        drain(2 * group)

    for copy in shared:
        copy.wait()


def correlate(slots, ids, spectra, out, tiles, sems):
    t = lax.axis_index("tm")
    lane = lax.broadcasted_iota(jnp.int32, (TB, LANES), 1)
    first = lane < LANES // 2
    even = lane // SPECTRA % 2 == 0
    for j in range(slots):
        number = ids[t * slots + j]
        row = jnp.int32(0)
        for k in range(1, 8):
            row = row + (number >= k * (k + 1) // 2).astype(jnp.int32)
        col = number - row * (row + 1) // 2
        left = spectra[pl.ds(pl.multiple_of(row * TB, TB), TB), :].astype(jnp.float32)
        right = spectra[pl.ds(pl.multiple_of(col * TB, TB), TB), :]
        turned = jnp.where(
            even,
            pltpu.roll(left, LANES - SPECTRA, 1),
            -pltpu.roll(left, SPECTRA, 1),
        )
        four = jnp.concatenate(
            [
                jnp.where(first, left, 0.0),
                jnp.where(first, turned, 0.0),
                jnp.where(first, 0.0, left),
                jnp.where(first, 0.0, turned),
            ],
            axis=0,
        ).astype(jnp.bfloat16)
        products = lax.dot_general(
            four, right, (((1,), (1,)), ((), ())), preferred_element_type=jnp.float32
        )
        tiles[j] = (products * (1.0 / SPECTRA)).reshape(CH_DEV, 2, TB, TB)
        pltpu.make_async_copy(tiles.at[j], out.at[j], sems.at[j]).start()
    for j in range(slots):
        pltpu.make_async_copy(tiles.at[j], out.at[j], sems.at[j]).wait()


def run_front(freqs, times, samples):
    rows = freqs // times // 2 * PATHS
    dma = pltpu.SemaphoreType.DMA
    hbm = pl.BlockSpec(memory_space=pl.ANY)
    tables = [
        window_table(),
        turn_table(),
        run_table(),
        quad_table(),
        place_table(times),
    ]
    return pl.pallas_call(
        functools.partial(front, freqs, times),
        out_shape=jax.ShapeDtypeStruct((freqs * PATHS, LANES), jnp.bfloat16),
        in_specs=[hbm] * (1 + len(tables)),
        out_specs=hbm,
        scratch_shapes=[
            pltpu.VMEM((PATHS * BLOCKS * ROWS, LANES), jnp.int32),
            *[pltpu.VMEM(table.shape, table.dtype) for table in tables],
            pltpu.VMEM((BATCH * OUT * HALF, 2 * LANES), jnp.bfloat16),
            pltpu.VMEM((PATHS * 2 * SLOT, LANES), jnp.float32),
            pltpu.VMEM((QUADS * PATHS, LANES), jnp.float32),
            pltpu.VMEM((QUADS * PATHS, LANES), jnp.bfloat16),
            pltpu.VMEM((times, rows, LANES), jnp.bfloat16),
            pltpu.VMEM((2, rows, LANES), jnp.bfloat16),
            dma((PATHS,)),
            dma((len(tables),)),
            dma((times - 1,)),
            dma((times - 1,)),
            dma,
            dma((PARTS,)),
            dma((PARTS,)),
            dma((PARTS,)),
        ],
        compiler_params=pltpu.CompilerParams(
            collective_id=0, has_side_effects=True, vmem_limit_bytes=60 * 2**20
        ),
        name="front",
    )(samples, *[jnp.asarray(table) for table in tables])


def run_correlate(slots, tile_map, spectra):
    return pl.pallas_call(
        functools.partial(correlate, slots),
        out_shape=jax.ShapeDtypeStruct((slots, CH_DEV, 2, TB, TB), jnp.float32),
        in_specs=[
            pl.BlockSpec(memory_space=pltpu.SMEM),
            pl.BlockSpec(memory_space=pltpu.VMEM),
        ],
        out_specs=pl.BlockSpec(memory_space=pl.ANY),
        scratch_shapes=[
            pltpu.VMEM((slots, CH_DEV, 2, TB, TB), jnp.float32),
            pltpu.SemaphoreType.DMA((slots,)),
        ],
        compiler_params=pltpu.CompilerParams(vmem_limit_bytes=40 * 2**20),
        name="correlate",
    )(tile_map, spectra)


def on_device(voltages, tile_map):
    freqs, times = lax.axis_size("freq"), lax.axis_size("tm")
    samples = voltages.reshape(PATHS, BLOCKS, 2, CHUNKS, LANES)
    samples = samples.transpose(0, 1, 3, 2, 4).reshape(PATHS * BLOCKS * ROWS, LANES)
    spectra = run_front(freqs, times, samples)
    return run_correlate(tile_map.shape[0] // times, tile_map, spectra)


def solution(mesh):
    in_specs = (P("freq", "tm", None, None), P())
    out_specs = P("tm", "freq", None, None, None)
    return jax.shard_map(
        on_device, mesh=mesh, in_specs=in_specs, out_specs=out_specs, check_vma=False
    )
```

```python
import functools
import math

import jax
import jax.numpy as jnp
import numpy as np
from jax import lax
from jax.experimental import pallas as pl
from jax.experimental.pallas import tpu as pltpu
from jax.sharding import PartitionSpec as P

NCHAN = 4096
TAPS = 4
TB = 128
CHANNELS = 128
FIRST = NCHAN // 2 - CHANNELS // 2
CH_DEV = 2
LANES = 128
CHUNKS = NCHAN // LANES
ROWS = 2 * CHUNKS
PARTIAL = 16
FOLD = ROWS // PARTIAL
BLOCKS = 8
OUT = BLOCKS + TAPS - 1
PATHS = 16
SLOT = 16
SPECTRA = 32
QUADS = CHANNELS // 4
BATCH = 8
PARTS = 4
MESH = pl.DeviceIdType.MESH


def window_table():
    n = np.arange(TAPS * NCHAN, dtype=np.float64) + 0.5
    taper = 0.5 - 0.5 * np.cos(2.0 * math.pi * n / (TAPS * NCHAN))
    taps = np.sinc(n / NCHAN - TAPS / 2.0) * taper / (128.0 * math.sqrt(NCHAN))
    taps = np.repeat(taps.reshape(TAPS, CHUNKS, 1, LANES), 2, axis=2)
    return taps.reshape(TAPS, ROWS, LANES).astype(np.float32)


def turn_table():
    sample = np.arange(LANES)[:, None]
    m = np.arange(CHANNELS)[None, :]
    angle = (sample * (FIRST + m) % NCHAN) * (2.0 * math.pi / NCHAN)
    real, imag = np.cos(angle), -np.sin(angle)
    quarters = []
    for h in range(FOLD):
        turns = h * (NCHAN // FOLD) * (FIRST + m) % NCHAN // (NCHAN // FOLD)
        cosine, sine = (np.array(v)[turns] for v in ((1, 0, -1, 0), (0, -1, 0, 1)))
        quarters.append(
            np.concatenate(
                [real * cosine - imag * sine, real * sine + imag * cosine], axis=1
            )
        )
    table = np.concatenate(quarters, axis=0).astype(np.float32)
    high = table.astype(jnp.bfloat16)
    low = (table - high.astype(np.float32)).astype(jnp.bfloat16)
    return np.concatenate([high, low], axis=0)


def run_table():
    run = np.arange(PARTIAL)[:, None] // 2
    part = np.arange(PARTIAL)[:, None] % 2
    m = np.arange(CHANNELS)[None, :]
    angle = (run * LANES * (FIRST + m) % NCHAN) * (2.0 * math.pi / NCHAN)
    turned = np.exp(-1j * angle) * np.where(part == 0, 1.0, 1j)
    return np.stack([turned.real, turned.imag]).astype(np.float32)


def quad_table():
    table = np.arange(QUADS)[:, None] == np.arange(CHANNELS)[None, :] // 4
    return table.astype(jnp.bfloat16)


def place_table(times):
    table = np.zeros((times, 2, 2, 2, SLOT, 2, 2, 2, SPECTRA), np.float32)
    for t in range(times):
        for step in range(OUT):
            if t * BLOCKS + step < times * BLOCKS:
                for e in range(2):
                    for c in range(2):
                        for q in range(2):
                            table[t, e, c, q, step, e, c, q, t * BLOCKS + step] = 1.0
    return table.reshape(times * LANES, 2 * LANES).astype(jnp.bfloat16)


def front(
    freqs,
    times,
    x_hbm,
    window_hbm,
    turn_hbm,
    runs_hbm,
    quads_hbm,
    place_hbm,
    spectra,
    x,
    window,
    turn,
    runs,
    quads,
    place,
    z,
    sums,
    mixed,
    packed,
    landed,
    ready,
    x_sem,
    table_sem,
    slice_send,
    slice_recv,
    spread_send,
    spread_recv,
    share_send,
    share_recv,
):
    f, t = lax.axis_index("freq"), lax.axis_index("tm")
    group = freqs // times
    rows = group // 2 * PATHS
    half = freqs // 2
    core, mine = f // half, lax.rem(t, 2)
    among = ((f // group == t) & (core == mine)).astype(jnp.int32)
    per_path = BLOCKS * ROWS

    def fetch(i):
        at = pl.ds(pl.multiple_of(i * per_path, per_path), per_path)
        return pltpu.make_async_copy(x_hbm.at[at], x.at[at], x_sem.at[i])

    def start_fetch(i, carry):
        fetch(i).start()
        return carry

    tables = [
        pltpu.make_async_copy(source, target, table_sem.at[k])
        for k, (source, target) in enumerate(
            zip(
                (window_hbm, turn_hbm, runs_hbm, quads_hbm, place_hbm),
                (window, turn, runs, quads, place),
            )
        )
    ]
    tables[0].start()
    lax.fori_loop(0, BATCH, start_fetch, 0)
    for table in tables[1:]:
        table.start()
    lax.fori_loop(BATCH, PATHS, start_fetch, 0)

    barrier = pltpu.get_barrier_semaphore()
    for d in range(1, times):
        pl.semaphore_signal(
            barrier, inc=1, device_id=(f, lax.rem(t + d, times)), device_id_type=MESH
        )

    def greet(j, carry):
        source = half * mine + j

        @pl.when((source != f) | (f // group != t))
        def _():
            pl.semaphore_signal(
                barrier, inc=1, device_id=(source, f // group), device_id_type=MESH
            )

        return carry

    lax.fori_loop(0, half, greet, 0)
    sums[...] = jnp.zeros_like(sums)

    tables[0].wait()

    def channelize(n, carry):
        def filtered(path, carry):
            fetch(n * BATCH + path).wait()
            for h in range(FOLD):
                start = (n * BATCH + path) * per_path + h * PARTIAL
                taps = [
                    window[k, h * PARTIAL : (h + 1) * PARTIAL, :] for k in range(TAPS)
                ]
                steps = [
                    x[
                        pl.ds(pl.multiple_of(start + b * ROWS, PARTIAL), PARTIAL), :
                    ].astype(jnp.float32)
                    for b in range(BLOCKS)
                ]
                for s in range(OUT):
                    terms = [
                        taps[k] * steps[s - TAPS + 1 + k]
                        for k in range(TAPS)
                        if 0 <= s - TAPS + 1 + k < BLOCKS
                    ]
                    total = functools.reduce(lambda a, b: a + b, terms)
                    at = pl.multiple_of((path * OUT + s) * PARTIAL, PARTIAL)
                    z[pl.ds(at, PARTIAL), h * LANES : (h + 1) * LANES] = total.astype(
                        jnp.bfloat16
                    )
            return carry

        lax.fori_loop(0, BATCH, filtered, 0)

        @pl.when(n == 0)
        def _():
            tables[1].wait()
            tables[2].wait()

        value = z[...]
        u = jnp.dot(
            jnp.concatenate([value, value], axis=1),
            turn[...],
            preferred_element_type=jnp.float32,
        )
        real, imag = runs[0], runs[1]
        for path in range(BATCH):
            at = pl.multiple_of((n * BATCH + path) * 2 * SLOT, 2 * SLOT)
            for s in range(OUT):
                k = (path * OUT + s) * PARTIAL
                u0, u1 = u[k : k + PARTIAL, :LANES], u[k : k + PARTIAL, LANES:]
                a = jnp.sum(real * u0 - imag * u1, axis=0, keepdims=True)
                b = jnp.sum(imag * u0 + real * u1, axis=0, keepdims=True)
                sums[pl.ds(at + s, 1), :] = a
                sums[pl.ds(at + SLOT + s, 1), :] = b
        return carry

    lax.fori_loop(0, PATHS // BATCH, channelize, 0)
    tables[3].wait()
    tables[4].wait()

    of_quad = lax.broadcasted_iota(jnp.int32, (2 * SLOT, LANES), 1) % 4
    for i in range(PATHS):
        value = sums[i * 2 * SLOT : (i + 1) * 2 * SLOT, :]
        four = jnp.concatenate(
            [jnp.where(of_quad == m, value, 0.0) for m in range(4)], axis=0
        ).astype(jnp.bfloat16)
        moved = lax.dot_general(
            quads[...],
            four,
            (((1,), (1,)), ((), ())),
            preferred_element_type=jnp.float32,
        )
        mixed[pl.ds(i, QUADS, stride=PATHS), :] = moved
    packed[...] = mixed[...].astype(jnp.bfloat16)

    pl.semaphore_wait(barrier, times - 1 + 2 * group - among)
    slices = []
    for d in range(1, times):
        to = lax.rem(t + d, times)
        copy = pltpu.make_async_remote_copy(
            src_ref=packed.at[pl.ds(pl.multiple_of(to * rows, rows), rows)],
            dst_ref=landed.at[t],
            send_sem=slice_send.at[d - 1],
            recv_sem=slice_recv.at[d - 1],
            device_id=(f, to),
            device_id_type=MESH,
        )
        copy.start()
        slices.append(copy)
    landed[t] = packed[pl.ds(pl.multiple_of(t * rows, rows), rows), :]
    for copy in slices:
        copy.wait_recv()

    joined = jnp.dot(
        jnp.concatenate([landed[j] for j in range(times)], axis=1),
        place[...],
        preferred_element_type=jnp.float32,
    ).astype(jnp.bfloat16)
    for e in range(2):
        ready[e] = joined[:, e * LANES : (e + 1) * LANES]

    here = spectra.at[pl.ds(pl.multiple_of(f * PATHS, PATHS), PATHS)]
    part = half // PARTS
    arrived = spread_recv.at[lax.rem(f // part, PARTS)]

    def spread(j, carry):
        k = lax.rem(j + f, 2 * group)
        number, time = k // 2, 2 * lax.rem(k, 2) + core
        at = pl.ds(pl.multiple_of(number // 2 * PATHS, PATHS), PATHS)
        tile = ready.at[lax.rem(number, 2), at]
        to = t * group + number
        local = (to == f) & (time == t)

        @pl.when(local)
        def _():
            pltpu.make_async_copy(tile, here, arrived).start()

        @pl.when(jnp.logical_not(local))
        def _():
            pltpu.make_async_remote_copy(
                src_ref=tile,
                dst_ref=here,
                send_sem=spread_send,
                recv_sem=arrived,
                device_id=(to, time),
                device_id_type=MESH,
            ).start()

        return carry

    lax.fori_loop(0, 2 * group, spread, 0)

    mate = t + 1 - 2 * mine
    shared = []
    for k in range(PARTS):
        at = (mine * PARTS + k) * part * PATHS
        some = spectra.at[pl.ds(pl.multiple_of(at, part * PATHS), part * PATHS)]
        pltpu.make_async_copy(some, some, spread_recv.at[k]).wait()
        copy = pltpu.make_async_remote_copy(
            src_ref=some,
            dst_ref=some,
            send_sem=share_send.at[k],
            recv_sem=share_recv.at[k],
            device_id=(f, mate),
            device_id_type=MESH,
        )
        copy.start()
        shared.append(copy)
    for copy in slices:
        copy.wait_send()

    def drain(count):
        some = spectra.at[pl.ds(0, count * PATHS)]
        pltpu.make_async_copy(some, some, spread_send).wait()

    @pl.when(among == 1)
    def _():
        drain(2 * group - 1)

    @pl.when(among == 0)
    def _():
        drain(2 * group)

    for copy in shared:
        copy.wait()


def correlate(slots, ids, spectra, out, tiles, sems):
    t = lax.axis_index("tm")
    lane = lax.broadcasted_iota(jnp.int32, (TB, LANES), 1)
    first = lane < LANES // 2
    even = lane // SPECTRA % 2 == 0
    for j in range(slots):
        number = ids[t * slots + j]
        row = jnp.int32(0)
        for k in range(1, 8):
            row = row + (number >= k * (k + 1) // 2).astype(jnp.int32)
        col = number - row * (row + 1) // 2
        left = spectra[pl.ds(pl.multiple_of(row * TB, TB), TB), :].astype(jnp.float32)
        right = spectra[pl.ds(pl.multiple_of(col * TB, TB), TB), :]
        turned = jnp.where(
            even,
            pltpu.roll(left, LANES - SPECTRA, 1),
            -pltpu.roll(left, SPECTRA, 1),
        )
        four = jnp.concatenate(
            [
                jnp.where(first, left, 0.0),
                jnp.where(first, turned, 0.0),
                jnp.where(first, 0.0, left),
                jnp.where(first, 0.0, turned),
            ],
            axis=0,
        ).astype(jnp.bfloat16)
        products = lax.dot_general(
            four, right, (((1,), (1,)), ((), ())), preferred_element_type=jnp.float32
        )
        tiles[j] = (products * (1.0 / SPECTRA)).reshape(CH_DEV, 2, TB, TB)
        pltpu.make_async_copy(tiles.at[j], out.at[j], sems.at[j]).start()
    for j in range(slots):
        pltpu.make_async_copy(tiles.at[j], out.at[j], sems.at[j]).wait()


def run_front(freqs, times, samples):
    rows = freqs // times // 2 * PATHS
    dma = pltpu.SemaphoreType.DMA
    hbm = pl.BlockSpec(memory_space=pl.ANY)
    tables = [
        window_table(),
        turn_table(),
        run_table(),
        quad_table(),
        place_table(times),
    ]
    return pl.pallas_call(
        functools.partial(front, freqs, times),
        out_shape=pltpu.VMEM((freqs * PATHS, LANES), jnp.bfloat16),
        in_specs=[hbm] * (1 + len(tables)),
        out_specs=hbm,
        scratch_shapes=[
            pltpu.VMEM((PATHS * BLOCKS * ROWS, LANES), jnp.int32),
            *[pltpu.VMEM(table.shape, table.dtype) for table in tables],
            pltpu.VMEM((BATCH * OUT * PARTIAL, FOLD * LANES), jnp.bfloat16),
            pltpu.VMEM((PATHS * 2 * SLOT, LANES), jnp.float32),
            pltpu.VMEM((QUADS * PATHS, LANES), jnp.float32),
            pltpu.VMEM((QUADS * PATHS, LANES), jnp.bfloat16),
            pltpu.VMEM((times, rows, LANES), jnp.bfloat16),
            pltpu.VMEM((2, rows, LANES), jnp.bfloat16),
            dma((PATHS,)),
            dma((len(tables),)),
            dma((times - 1,)),
            dma((times - 1,)),
            dma,
            dma((PARTS,)),
            dma((PARTS,)),
            dma((PARTS,)),
        ],
        compiler_params=pltpu.CompilerParams(
            collective_id=0, has_side_effects=True, vmem_limit_bytes=60 * 2**20
        ),
        name="front",
    )(samples, *[jnp.asarray(table) for table in tables])


def run_correlate(slots, tile_map, spectra):
    return pl.pallas_call(
        functools.partial(correlate, slots),
        out_shape=jax.ShapeDtypeStruct((slots, CH_DEV, 2, TB, TB), jnp.float32),
        in_specs=[
            pl.BlockSpec(memory_space=pltpu.SMEM),
            pl.BlockSpec(memory_space=pltpu.VMEM),
        ],
        out_specs=pl.BlockSpec(memory_space=pl.ANY),
        scratch_shapes=[
            pltpu.VMEM((slots, CH_DEV, 2, TB, TB), jnp.float32),
            pltpu.SemaphoreType.DMA((slots,)),
        ],
        compiler_params=pltpu.CompilerParams(vmem_limit_bytes=40 * 2**20),
        name="correlate",
    )(tile_map, spectra)


def on_device(voltages, tile_map):
    freqs, times = lax.axis_size("freq"), lax.axis_size("tm")
    samples = voltages.reshape(PATHS, BLOCKS, 2, CHUNKS, LANES)
    samples = samples.transpose(0, 1, 3, 2, 4).reshape(PATHS * BLOCKS * ROWS, LANES)
    spectra = run_front(freqs, times, samples)
    return run_correlate(tile_map.shape[0] // times, tile_map, spectra)


def solution(mesh):
    in_specs = (P("freq", "tm", None, None), P())
    out_specs = P("tm", "freq", None, None, None)
    return jax.shard_map(
        on_device, mesh=mesh, in_specs=in_specs, out_specs=out_specs, check_vma=False
    )
```

```python
import functools
import math

import jax
import jax.numpy as jnp
import numpy as np
from jax import lax
from jax.experimental import pallas as pl
from jax.experimental.pallas import tpu as pltpu
from jax.sharding import PartitionSpec as P

NCHAN = 4096
TAPS = 4
TB = 128
CHANNELS = 128
FIRST = NCHAN // 2 - CHANNELS // 2
CH_DEV = 2
LANES = 128
CHUNKS = NCHAN // LANES
ROWS = 2 * CHUNKS
PARTIAL = 16
FOLD = ROWS // PARTIAL
BLOCKS = 8
OUT = BLOCKS + TAPS - 1
PATHS = 16
SLOT = 16
SPECTRA = 32
QUADS = CHANNELS // 4
BATCH = 8
PIECES = 2
PARTS = 4
MESH = pl.DeviceIdType.MESH


def window_table():
    n = np.arange(TAPS * NCHAN, dtype=np.float64) + 0.5
    taper = 0.5 - 0.5 * np.cos(2.0 * math.pi * n / (TAPS * NCHAN))
    taps = np.sinc(n / NCHAN - TAPS / 2.0) * taper / (128.0 * math.sqrt(NCHAN))
    taps = np.repeat(taps.reshape(TAPS, CHUNKS, 1, LANES), 2, axis=2)
    return taps.reshape(TAPS, ROWS, LANES).astype(np.float32)


def turn_table():
    sample = np.arange(LANES)[:, None]
    m = np.arange(CHANNELS)[None, :]
    angle = (sample * (FIRST + m) % NCHAN) * (2.0 * math.pi / NCHAN)
    real, imag = np.cos(angle), -np.sin(angle)
    quarters = []
    for h in range(FOLD):
        turns = h * (NCHAN // FOLD) * (FIRST + m) % NCHAN // (NCHAN // FOLD)
        cosine, sine = (np.array(v)[turns] for v in ((1, 0, -1, 0), (0, -1, 0, 1)))
        quarters.append(
            np.concatenate(
                [real * cosine - imag * sine, real * sine + imag * cosine], axis=1
            )
        )
    table = np.concatenate(quarters, axis=0).astype(np.float32)
    high = table.astype(jnp.bfloat16)
    low = (table - high.astype(np.float32)).astype(jnp.bfloat16)
    return np.concatenate([high, low], axis=0)


def run_table():
    run = np.arange(PARTIAL)[:, None] // 2
    part = np.arange(PARTIAL)[:, None] % 2
    m = np.arange(CHANNELS)[None, :]
    angle = (run * LANES * (FIRST + m) % NCHAN) * (2.0 * math.pi / NCHAN)
    turned = np.exp(-1j * angle) * np.where(part == 0, 1.0, 1j)
    return np.stack([turned.real, turned.imag]).astype(np.float32)


def quad_table():
    table = np.arange(QUADS)[:, None] == np.arange(CHANNELS)[None, :] // 4
    return table.astype(jnp.bfloat16)


def place_table(times):
    table = np.zeros((times, 2, 2, 2, SLOT, 2, 2, 2, SPECTRA), np.float32)
    for t in range(times):
        for step in range(OUT):
            if t * BLOCKS + step < times * BLOCKS:
                for e in range(2):
                    for c in range(2):
                        for q in range(2):
                            table[t, e, c, q, step, e, c, q, t * BLOCKS + step] = 1.0
    return table.reshape(times * LANES, 2 * LANES).astype(jnp.bfloat16)


def front(
    freqs,
    times,
    x_hbm,
    window_hbm,
    turn_hbm,
    runs_hbm,
    quads_hbm,
    place_hbm,
    spectra,
    x,
    window,
    turn,
    runs,
    quads,
    place,
    z,
    sums,
    mixed,
    packed,
    landed,
    ready,
    x_sem,
    table_sem,
    slice_send,
    slice_recv,
    spread_send,
    spread_recv,
    share_send,
    share_recv,
):
    f, t = lax.axis_index("freq"), lax.axis_index("tm")
    group = freqs // times
    rows = group // 2 * PATHS
    half = freqs // 2
    core, mine = f // half, lax.rem(t, 2)
    among = ((f // group == t) & (core == mine)).astype(jnp.int32)
    per_path = BLOCKS * ROWS

    def fetch(i):
        at = pl.ds(pl.multiple_of(i * per_path, per_path), per_path)
        return pltpu.make_async_copy(x_hbm.at[at], x.at[at], x_sem.at[i])

    def start_fetch(i, carry):
        fetch(i).start()
        return carry

    tables = [
        pltpu.make_async_copy(source, target, table_sem.at[k])
        for k, (source, target) in enumerate(
            zip(
                (window_hbm, turn_hbm, runs_hbm, quads_hbm, place_hbm),
                (window, turn, runs, quads, place),
            )
        )
    ]
    tables[0].start()
    lax.fori_loop(0, BATCH, start_fetch, 0)
    for table in tables[1:]:
        table.start()
    lax.fori_loop(BATCH, PATHS, start_fetch, 0)

    barrier = pltpu.get_barrier_semaphore()
    for d in range(1, times):
        pl.semaphore_signal(
            barrier, inc=1, device_id=(f, lax.rem(t + d, times)), device_id_type=MESH
        )

    def greet(j, carry):
        source = half * mine + j

        @pl.when((source != f) | (f // group != t))
        def _():
            pl.semaphore_signal(
                barrier, inc=1, device_id=(source, f // group), device_id_type=MESH
            )

        return carry

    lax.fori_loop(0, half, greet, 0)
    sums[...] = jnp.zeros_like(sums)

    tables[0].wait()

    def channelize(n, carry):
        def filtered(path, carry):
            fetch(n * BATCH + path).wait()
            for h in range(FOLD):
                start = (n * BATCH + path) * per_path + h * PARTIAL
                taps = [
                    window[k, h * PARTIAL : (h + 1) * PARTIAL, :] for k in range(TAPS)
                ]
                steps = [
                    x[
                        pl.ds(pl.multiple_of(start + b * ROWS, PARTIAL), PARTIAL), :
                    ].astype(jnp.float32)
                    for b in range(BLOCKS)
                ]
                for s in range(OUT):
                    terms = [
                        taps[k] * steps[s - TAPS + 1 + k]
                        for k in range(TAPS)
                        if 0 <= s - TAPS + 1 + k < BLOCKS
                    ]
                    total = functools.reduce(lambda a, b: a + b, terms)
                    at = pl.multiple_of((path * OUT + s) * PARTIAL, PARTIAL)
                    z[pl.ds(at, PARTIAL), h * LANES : (h + 1) * LANES] = total.astype(
                        jnp.bfloat16
                    )
            return carry

        lax.fori_loop(0, BATCH, filtered, 0)

        @pl.when(n == 0)
        def _():
            tables[1].wait()
            tables[2].wait()

        value = z[...]
        u = jnp.dot(
            jnp.concatenate([value, value], axis=1),
            turn[...],
            preferred_element_type=jnp.float32,
        )
        real, imag = runs[0], runs[1]
        for path in range(BATCH):
            at = pl.multiple_of((n * BATCH + path) * 2 * SLOT, 2 * SLOT)
            for s in range(OUT):
                k = (path * OUT + s) * PARTIAL
                u0, u1 = u[k : k + PARTIAL, :LANES], u[k : k + PARTIAL, LANES:]
                a = jnp.sum(real * u0 - imag * u1, axis=0, keepdims=True)
                b = jnp.sum(imag * u0 + real * u1, axis=0, keepdims=True)
                sums[pl.ds(at + s, 1), :] = a
                sums[pl.ds(at + SLOT + s, 1), :] = b
        return carry

    lax.fori_loop(0, PATHS // BATCH, channelize, 0)
    tables[3].wait()
    tables[4].wait()

    of_quad = lax.broadcasted_iota(jnp.int32, (2 * SLOT, LANES), 1) % 4
    for i in range(PATHS):
        value = sums[i * 2 * SLOT : (i + 1) * 2 * SLOT, :]
        four = jnp.concatenate(
            [jnp.where(of_quad == m, value, 0.0) for m in range(4)], axis=0
        ).astype(jnp.bfloat16)
        moved = lax.dot_general(
            quads[...],
            four,
            (((1,), (1,)), ((), ())),
            preferred_element_type=jnp.float32,
        )
        mixed[pl.ds(i, QUADS, stride=PATHS), :] = moved
    columns = group // 2
    z_here = lax.rem(f // 2, columns)
    far_first = [
        lax.rem(z_here + d, columns)
        for d in sorted(range(columns), key=lambda d: -min(d, columns - d))
    ]
    for to in range(times):
        for n, column in enumerate(far_first):
            at = pl.multiple_of((to * columns + column) * PATHS, PATHS)
            tile = mixed[pl.ds(at, PATHS), :]
            at = to * rows + n * PATHS
            packed[at : at + PATHS, :] = tile.astype(jnp.bfloat16)

    pl.semaphore_wait(barrier, times - 1 + 2 * group - among)
    piece = rows // PIECES
    slices = [[] for _ in range(PIECES)]
    for p in range(PIECES):
        for d in (2, 3, 1):
            to = t + d - 2 * (t & d)
            k = p * (times - 1) + d - 1
            at = pl.multiple_of(to * rows + p * piece, piece)
            copy = pltpu.make_async_remote_copy(
                src_ref=packed.at[pl.ds(at, piece)],
                dst_ref=landed.at[p, t],
                send_sem=slice_send.at[k],
                recv_sem=slice_recv.at[k],
                device_id=(f, to),
                device_id_type=MESH,
            )
            copy.start()
            slices[p].append(copy)
    for p in range(PIECES):
        at = pl.multiple_of(t * rows + p * piece, piece)
        landed[p, t] = packed[pl.ds(at, piece), :]

    here = spectra.at[pl.ds(pl.multiple_of(f * PATHS, PATHS), PATHS)]
    part = half // PARTS
    arrived = spread_recv.at[lax.rem(f // part, PARTS)]

    for p in range(PIECES):
        for copy in slices[p]:
            copy.wait_recv()
        joined = jnp.dot(
            jnp.concatenate([landed[p, j] for j in range(times)], axis=1),
            place[...],
            preferred_element_type=jnp.float32,
        ).astype(jnp.bfloat16)
        for e in range(2):
            ready[e, p * piece : (p + 1) * piece, :] = joined[
                :, e * LANES : (e + 1) * LANES
            ]
        for n in range(p * columns // PIECES, (p + 1) * columns // PIECES):
            for e in range(2):
                to = t * group + far_first[n] * 2 + e
                tile = ready.at[e, pl.ds(n * PATHS, PATHS)]
                for across in range(2):
                    time = 2 * across + core
                    copy = pltpu.make_async_remote_copy(
                        src_ref=tile,
                        dst_ref=here,
                        send_sem=spread_send,
                        recv_sem=arrived,
                        device_id=(to, time),
                        device_id_type=MESH,
                    )
                    if n < columns - 1:
                        copy.start()
                        continue
                    local = (to == f) & (time == t)
                    pl.when(jnp.logical_not(local))(copy.start)
                    pl.when(local)(pltpu.make_async_copy(tile, here, arrived).start)

    mate = t + 1 - 2 * mine
    shared = []
    for k in range(PARTS):
        at = (mine * PARTS + k) * part * PATHS
        some = spectra.at[pl.ds(pl.multiple_of(at, part * PATHS), part * PATHS)]
        pltpu.make_async_copy(some, some, spread_recv.at[k]).wait()
        copy = pltpu.make_async_remote_copy(
            src_ref=some,
            dst_ref=some,
            send_sem=share_send.at[k],
            recv_sem=share_recv.at[k],
            device_id=(f, mate),
            device_id_type=MESH,
        )
        copy.start()
        shared.append(copy)
    for copy in sum(slices, []):
        copy.wait_send()

    def drain(count):
        some = spectra.at[pl.ds(0, count * PATHS)]
        pltpu.make_async_copy(some, some, spread_send).wait()

    @pl.when(among == 1)
    def _():
        drain(2 * group - 1)

    @pl.when(among == 0)
    def _():
        drain(2 * group)

    for copy in shared:
        copy.wait()


def correlate(slots, ids, spectra, out, tiles, sems):
    t = lax.axis_index("tm")
    lane = lax.broadcasted_iota(jnp.int32, (TB, LANES), 1)
    first = lane < LANES // 2
    even = lane // SPECTRA % 2 == 0
    for j in range(slots):
        number = ids[t * slots + j]
        row = jnp.int32(0)
        for k in range(1, 8):
            row = row + (number >= k * (k + 1) // 2).astype(jnp.int32)
        col = number - row * (row + 1) // 2
        left = spectra[pl.ds(pl.multiple_of(row * TB, TB), TB), :].astype(jnp.float32)
        right = spectra[pl.ds(pl.multiple_of(col * TB, TB), TB), :]
        turned = jnp.where(
            even,
            pltpu.roll(left, LANES - SPECTRA, 1),
            -pltpu.roll(left, SPECTRA, 1),
        )
        four = jnp.concatenate(
            [
                jnp.where(first, left, 0.0),
                jnp.where(first, turned, 0.0),
                jnp.where(first, 0.0, left),
                jnp.where(first, 0.0, turned),
            ],
            axis=0,
        ).astype(jnp.bfloat16)
        products = lax.dot_general(
            four, right, (((1,), (1,)), ((), ())), preferred_element_type=jnp.float32
        )
        tiles[j] = (products * (1.0 / SPECTRA)).reshape(CH_DEV, 2, TB, TB)
        pltpu.make_async_copy(tiles.at[j], out.at[j], sems.at[j]).start()
    for j in range(slots):
        pltpu.make_async_copy(tiles.at[j], out.at[j], sems.at[j]).wait()


def run_front(freqs, times, samples):
    rows = freqs // times // 2 * PATHS
    dma = pltpu.SemaphoreType.DMA
    hbm = pl.BlockSpec(memory_space=pl.ANY)
    tables = [
        window_table(),
        turn_table(),
        run_table(),
        quad_table(),
        place_table(times),
    ]
    return pl.pallas_call(
        functools.partial(front, freqs, times),
        out_shape=pltpu.VMEM((freqs * PATHS, LANES), jnp.bfloat16),
        in_specs=[hbm] * (1 + len(tables)),
        out_specs=hbm,
        scratch_shapes=[
            pltpu.VMEM((PATHS * BLOCKS * ROWS, LANES), jnp.int32),
            *[pltpu.VMEM(table.shape, table.dtype) for table in tables],
            pltpu.VMEM((BATCH * OUT * PARTIAL, FOLD * LANES), jnp.bfloat16),
            pltpu.VMEM((PATHS * 2 * SLOT, LANES), jnp.float32),
            pltpu.VMEM((QUADS * PATHS, LANES), jnp.float32),
            pltpu.VMEM((QUADS * PATHS, LANES), jnp.bfloat16),
            pltpu.VMEM((PIECES, times, rows // PIECES, LANES), jnp.bfloat16),
            pltpu.VMEM((2, rows, LANES), jnp.bfloat16),
            dma((PATHS,)),
            dma((len(tables),)),
            dma((PIECES * (times - 1),)),
            dma((PIECES * (times - 1),)),
            dma,
            dma((PARTS,)),
            dma((PARTS,)),
            dma((PARTS,)),
        ],
        compiler_params=pltpu.CompilerParams(
            collective_id=0, has_side_effects=True, vmem_limit_bytes=60 * 2**20
        ),
        name="front",
    )(samples, *[jnp.asarray(table) for table in tables])


def run_correlate(slots, tile_map, spectra):
    return pl.pallas_call(
        functools.partial(correlate, slots),
        out_shape=jax.ShapeDtypeStruct((slots, CH_DEV, 2, TB, TB), jnp.float32),
        in_specs=[
            pl.BlockSpec(memory_space=pltpu.SMEM),
            pl.BlockSpec(memory_space=pltpu.VMEM),
        ],
        out_specs=pl.BlockSpec(memory_space=pl.ANY),
        scratch_shapes=[
            pltpu.VMEM((slots, CH_DEV, 2, TB, TB), jnp.float32),
            pltpu.SemaphoreType.DMA((slots,)),
        ],
        compiler_params=pltpu.CompilerParams(vmem_limit_bytes=40 * 2**20),
        name="correlate",
    )(tile_map, spectra)


def on_device(voltages, tile_map):
    freqs, times = lax.axis_size("freq"), lax.axis_size("tm")
    samples = voltages.reshape(PATHS, BLOCKS, 2, CHUNKS, LANES)
    samples = samples.transpose(0, 1, 3, 2, 4).reshape(PATHS * BLOCKS * ROWS, LANES)
    spectra = run_front(freqs, times, samples)
    return run_correlate(tile_map.shape[0] // times, tile_map, spectra)


def solution(mesh):
    in_specs = (P("freq", "tm", None, None), P())
    out_specs = P("tm", "freq", None, None, None)
    return jax.shard_map(
        on_device, mesh=mesh, in_specs=in_specs, out_specs=out_specs, check_vma=False
    )
```

```python
import functools
import math

import jax
import jax.numpy as jnp
import numpy as np
from jax import lax
from jax.experimental import pallas as pl
from jax.experimental.pallas import tpu as pltpu
from jax.sharding import PartitionSpec as P

NCHAN = 4096
TAPS = 4
TB = 128
CHANNELS = 128
FIRST = NCHAN // 2 - CHANNELS // 2
CH_DEV = 2
LANES = 128
CHUNKS = NCHAN // LANES
ROWS = 2 * CHUNKS
PARTIAL = 16
FOLD = ROWS // PARTIAL
BLOCKS = 8
OUT = BLOCKS + TAPS - 1
PATHS = 16
SLOT = 16
SPECTRA = 32
QUADS = CHANNELS // 4
BATCH = 8
PIECES = 2
PARTS = 4
MESH = pl.DeviceIdType.MESH


def window_table():
    n = np.arange(TAPS * NCHAN, dtype=np.float64) + 0.5
    taper = 0.5 - 0.5 * np.cos(2.0 * math.pi * n / (TAPS * NCHAN))
    taps = np.sinc(n / NCHAN - TAPS / 2.0) * taper / (128.0 * math.sqrt(NCHAN))
    taps = np.repeat(taps.reshape(TAPS, CHUNKS, 1, LANES), 2, axis=2)
    return taps.reshape(TAPS, ROWS, LANES).astype(np.float32)


def turn_table():
    sample = np.arange(LANES)[:, None]
    m = np.arange(CHANNELS)[None, :]
    angle = (sample * (FIRST + m) % NCHAN) * (2.0 * math.pi / NCHAN)
    real, imag = np.cos(angle), -np.sin(angle)
    quarters = []
    for h in range(FOLD):
        turns = h * (NCHAN // FOLD) * (FIRST + m) % NCHAN // (NCHAN // FOLD)
        cosine, sine = (np.array(v)[turns] for v in ((1, 0, -1, 0), (0, -1, 0, 1)))
        quarters.append(
            np.concatenate(
                [real * cosine - imag * sine, real * sine + imag * cosine], axis=1
            )
        )
    return np.concatenate(quarters, axis=0).astype(np.float32).astype(jnp.bfloat16)


def run_table():
    run = np.arange(PARTIAL)[:, None] // 2
    part = np.arange(PARTIAL)[:, None] % 2
    m = np.arange(CHANNELS)[None, :]
    angle = (run * LANES * (FIRST + m) % NCHAN) * (2.0 * math.pi / NCHAN)
    turned = np.exp(-1j * angle) * np.where(part == 0, 1.0, 1j)
    return np.stack([turned.real, turned.imag]).astype(np.float32)


def quad_table():
    table = np.arange(QUADS)[:, None] == np.arange(CHANNELS)[None, :] // 4
    return table.astype(jnp.bfloat16)


def place_table(times):
    table = np.zeros((times, 2, 2, 2, SLOT, 2, 2, 2, SPECTRA), np.float32)
    for t in range(times):
        for step in range(OUT):
            if t * BLOCKS + step < times * BLOCKS:
                for e in range(2):
                    for c in range(2):
                        for q in range(2):
                            table[t, e, c, q, step, e, c, q, t * BLOCKS + step] = 1.0
    return table.reshape(times * LANES, 2 * LANES).astype(jnp.bfloat16)


def front(
    freqs,
    times,
    x_hbm,
    window_hbm,
    turn_hbm,
    runs_hbm,
    quads_hbm,
    place_hbm,
    spectra,
    x,
    window,
    turn,
    runs,
    quads,
    place,
    z,
    sums,
    mixed,
    packed,
    landed,
    ready,
    x_sem,
    table_sem,
    slice_send,
    slice_recv,
    spread_send,
    spread_recv,
    share_send,
    share_recv,
):
    f, t = lax.axis_index("freq"), lax.axis_index("tm")
    group = freqs // times
    rows = group // 2 * PATHS
    half = freqs // 2
    core, mine = f // half, lax.rem(t, 2)
    among = ((f // group == t) & (core == mine)).astype(jnp.int32)
    per_path = BLOCKS * ROWS

    def fetch(i):
        at = pl.ds(pl.multiple_of(i * per_path, per_path), per_path)
        return pltpu.make_async_copy(x_hbm.at[at], x.at[at], x_sem.at[i])

    def start_fetch(i, carry):
        fetch(i).start()
        return carry

    tables = [
        pltpu.make_async_copy(source, target, table_sem.at[k])
        for k, (source, target) in enumerate(
            zip(
                (window_hbm, turn_hbm, runs_hbm, quads_hbm, place_hbm),
                (window, turn, runs, quads, place),
            )
        )
    ]
    tables[0].start()
    lax.fori_loop(0, BATCH, start_fetch, 0)
    for table in tables[1:4]:
        table.start()
    lax.fori_loop(BATCH, PATHS, start_fetch, 0)
    tables[4].start()

    barrier = pltpu.get_barrier_semaphore()
    for d in range(1, times):
        pl.semaphore_signal(
            barrier, inc=1, device_id=(f, lax.rem(t + d, times)), device_id_type=MESH
        )

    def greet(j, carry):
        source = half * mine + j

        @pl.when((source != f) | (f // group != t))
        def _():
            pl.semaphore_signal(
                barrier, inc=1, device_id=(source, f // group), device_id_type=MESH
            )

        return carry

    lax.fori_loop(0, half, greet, 0)
    sums[...] = jnp.zeros_like(sums)

    tables[0].wait()

    def channelize(n, carry):
        def filtered(path, carry):
            fetch(n * BATCH + path).wait()
            for h in range(FOLD):
                start = (n * BATCH + path) * per_path + h * PARTIAL
                taps = [
                    window[k, h * PARTIAL : (h + 1) * PARTIAL, :] for k in range(TAPS)
                ]
                steps = [
                    x[
                        pl.ds(pl.multiple_of(start + b * ROWS, PARTIAL), PARTIAL), :
                    ].astype(jnp.float32)
                    for b in range(BLOCKS)
                ]
                for s in range(OUT):
                    terms = [
                        taps[k] * steps[s - TAPS + 1 + k]
                        for k in range(TAPS)
                        if 0 <= s - TAPS + 1 + k < BLOCKS
                    ]
                    total = functools.reduce(lambda a, b: a + b, terms)
                    at = pl.multiple_of((path * OUT + s) * PARTIAL, PARTIAL)
                    z[pl.ds(at, PARTIAL), h * LANES : (h + 1) * LANES] = total.astype(
                        jnp.bfloat16
                    )
            return carry

        lax.fori_loop(0, BATCH, filtered, 0)

        @pl.when(n == 0)
        def _():
            for table in tables[1:3]:
                table.wait()

        u = jnp.dot(z[...], turn[...], preferred_element_type=jnp.float32)
        real, imag = runs[0], runs[1]
        for path in range(BATCH):
            at = pl.multiple_of((n * BATCH + path) * 2 * SLOT, 2 * SLOT)
            for s in range(OUT):
                k = (path * OUT + s) * PARTIAL
                u0, u1 = u[k : k + PARTIAL, :LANES], u[k : k + PARTIAL, LANES:]
                a = jnp.sum(real * u0 - imag * u1, axis=0, keepdims=True)
                b = jnp.sum(imag * u0 + real * u1, axis=0, keepdims=True)
                sums[pl.ds(at + s, 1), :] = a
                sums[pl.ds(at + SLOT + s, 1), :] = b
        return carry

    lax.fori_loop(0, PATHS // BATCH, channelize, 0)
    tables[3].wait()
    tables[4].wait()

    of_quad = lax.broadcasted_iota(jnp.int32, (2 * SLOT, LANES), 1) % 4
    for i in range(PATHS):
        value = sums[i * 2 * SLOT : (i + 1) * 2 * SLOT, :]
        four = jnp.concatenate(
            [jnp.where(of_quad == m, value, 0.0) for m in range(4)], axis=0
        ).astype(jnp.bfloat16)
        moved = lax.dot_general(
            quads[...],
            four,
            (((1,), (1,)), ((), ())),
            preferred_element_type=jnp.float32,
        )
        mixed[pl.ds(i, QUADS, stride=PATHS), :] = moved

    columns = group // 2
    z_here = lax.rem(f // 2, columns)
    far_first = [
        lax.rem(z_here + d, columns)
        for d in sorted(range(columns), key=lambda d: -min(d, columns - d))
    ]
    for to in range(times):
        for n, column in enumerate(far_first):
            at = pl.multiple_of((to * columns + column) * PATHS, PATHS)
            tile = mixed[pl.ds(at, PATHS), :]
            at = to * rows + n * PATHS
            packed[at : at + PATHS, :] = tile.astype(jnp.bfloat16)

    pl.semaphore_wait(barrier, times - 1 + 2 * group - among)
    piece = rows // PIECES
    slices = [[] for _ in range(PIECES)]
    for p in range(PIECES):
        for d in (2, 3, 1):
            to = t + d - 2 * (t & d)
            k = p * (times - 1) + d - 1
            at = pl.multiple_of(to * rows + p * piece, piece)
            copy = pltpu.make_async_remote_copy(
                src_ref=packed.at[pl.ds(at, piece)],
                dst_ref=landed.at[p, t],
                send_sem=slice_send.at[k],
                recv_sem=slice_recv.at[k],
                device_id=(f, to),
                device_id_type=MESH,
            )
            copy.start()
            slices[p].append(copy)
    for p in range(PIECES):
        at = pl.multiple_of(t * rows + p * piece, piece)
        landed[p, t] = packed[pl.ds(at, piece), :]

    here = spectra.at[pl.ds(pl.multiple_of(f * PATHS, PATHS), PATHS)]
    part = half // PARTS
    arrived = spread_recv.at[lax.rem(f // part, PARTS)]

    for p in range(PIECES):
        for copy in slices[p]:
            copy.wait_recv()
        joined = jnp.dot(
            jnp.concatenate([landed[p, j] for j in range(times)], axis=1),
            place[...],
            preferred_element_type=jnp.float32,
        ).astype(jnp.bfloat16)
        for e in range(2):
            ready[e, p * piece : (p + 1) * piece, :] = joined[
                :, e * LANES : (e + 1) * LANES
            ]
        for n in range(p * columns // PIECES, (p + 1) * columns // PIECES):
            for e in range(2):
                to = t * group + far_first[n] * 2 + e
                tile = ready.at[e, pl.ds(n * PATHS, PATHS)]
                for across in range(2):
                    time = 2 * across + core
                    copy = pltpu.make_async_remote_copy(
                        src_ref=tile,
                        dst_ref=here,
                        send_sem=spread_send,
                        recv_sem=arrived,
                        device_id=(to, time),
                        device_id_type=MESH,
                    )
                    if n < columns - 1:
                        copy.start()
                        continue
                    local = (to == f) & (time == t)
                    pl.when(jnp.logical_not(local))(copy.start)
                    pl.when(local)(pltpu.make_async_copy(tile, here, arrived).start)

    mate = t + 1 - 2 * mine
    shared = []
    for k in range(PARTS):
        at = (mine * PARTS + k) * part * PATHS
        some = spectra.at[pl.ds(pl.multiple_of(at, part * PATHS), part * PATHS)]
        pltpu.make_async_copy(some, some, spread_recv.at[k]).wait()
        copy = pltpu.make_async_remote_copy(
            src_ref=some,
            dst_ref=some,
            send_sem=share_send.at[k],
            recv_sem=share_recv.at[k],
            device_id=(f, mate),
            device_id_type=MESH,
        )
        copy.start()
        shared.append(copy)
    for copy in sum(slices, []):
        copy.wait_send()

    def drain(count):
        some = spectra.at[pl.ds(0, count * PATHS)]
        pltpu.make_async_copy(some, some, spread_send).wait()

    @pl.when(among == 1)
    def _():
        drain(2 * group - 1)

    @pl.when(among == 0)
    def _():
        drain(2 * group)

    for copy in shared:
        copy.wait()


def correlate(slots, ids, spectra, out, tiles, sems):
    t = lax.axis_index("tm")
    lane = lax.broadcasted_iota(jnp.int32, (TB, LANES), 1)
    first = lane < LANES // 2
    even = lane // SPECTRA % 2 == 0
    for j in range(slots):
        number = ids[t * slots + j]
        row = jnp.int32(0)
        for k in range(1, 8):
            row = row + (number >= k * (k + 1) // 2).astype(jnp.int32)
        col = number - row * (row + 1) // 2
        left = spectra[pl.ds(pl.multiple_of(row * TB, TB), TB), :].astype(jnp.float32)
        right = spectra[pl.ds(pl.multiple_of(col * TB, TB), TB), :]
        turned = jnp.where(
            even,
            pltpu.roll(left, LANES - SPECTRA, 1),
            -pltpu.roll(left, SPECTRA, 1),
        )
        four = jnp.concatenate(
            [
                jnp.where(first, left, 0.0),
                jnp.where(first, turned, 0.0),
                jnp.where(first, 0.0, left),
                jnp.where(first, 0.0, turned),
            ],
            axis=0,
        ).astype(jnp.bfloat16)
        products = lax.dot_general(
            four, right, (((1,), (1,)), ((), ())), preferred_element_type=jnp.float32
        )
        tiles[j] = (products * (1.0 / SPECTRA)).reshape(CH_DEV, 2, TB, TB)
        pltpu.make_async_copy(tiles.at[j], out.at[j], sems.at[j]).start()
    for j in range(slots):
        pltpu.make_async_copy(tiles.at[j], out.at[j], sems.at[j]).wait()


def run_front(freqs, times, samples):
    rows = freqs // times // 2 * PATHS
    dma = pltpu.SemaphoreType.DMA
    hbm = pl.BlockSpec(memory_space=pl.ANY)
    tables = [
        window_table(),
        turn_table(),
        run_table(),
        quad_table(),
        place_table(times),
    ]
    return pl.pallas_call(
        functools.partial(front, freqs, times),
        out_shape=pltpu.VMEM((freqs * PATHS, LANES), jnp.bfloat16),
        in_specs=[hbm] * (1 + len(tables)),
        out_specs=hbm,
        scratch_shapes=[
            pltpu.VMEM((PATHS * BLOCKS * ROWS, LANES), jnp.int32),
            *[pltpu.VMEM(table.shape, table.dtype) for table in tables],
            pltpu.VMEM((BATCH * OUT * PARTIAL, FOLD * LANES), jnp.bfloat16),
            pltpu.VMEM((PATHS * 2 * SLOT, LANES), jnp.float32),
            pltpu.VMEM((QUADS * PATHS, LANES), jnp.float32),
            pltpu.VMEM((QUADS * PATHS, LANES), jnp.bfloat16),
            pltpu.VMEM((PIECES, times, rows // PIECES, LANES), jnp.bfloat16),
            pltpu.VMEM((2, rows, LANES), jnp.bfloat16),
            dma((PATHS,)),
            dma((len(tables),)),
            dma((PIECES * (times - 1),)),
            dma((PIECES * (times - 1),)),
            dma,
            dma((PARTS,)),
            dma((PARTS,)),
            dma((PARTS,)),
        ],
        compiler_params=pltpu.CompilerParams(
            collective_id=0, has_side_effects=True, vmem_limit_bytes=60 * 2**20
        ),
        name="front",
    )(samples, *[jnp.asarray(table) for table in tables])


def run_correlate(slots, tile_map, spectra):
    return pl.pallas_call(
        functools.partial(correlate, slots),
        out_shape=jax.ShapeDtypeStruct((slots, CH_DEV, 2, TB, TB), jnp.float32),
        in_specs=[
            pl.BlockSpec(memory_space=pltpu.SMEM),
            pl.BlockSpec(memory_space=pltpu.VMEM),
        ],
        out_specs=pl.BlockSpec(memory_space=pl.ANY),
        scratch_shapes=[
            pltpu.VMEM((slots, CH_DEV, 2, TB, TB), jnp.float32),
            pltpu.SemaphoreType.DMA((slots,)),
        ],
        compiler_params=pltpu.CompilerParams(vmem_limit_bytes=40 * 2**20),
        name="correlate",
    )(tile_map, spectra)


def on_device(voltages, tile_map):
    freqs, times = lax.axis_size("freq"), lax.axis_size("tm")
    samples = voltages.reshape(PATHS, BLOCKS, 2, CHUNKS, LANES)
    samples = samples.transpose(0, 1, 3, 2, 4).reshape(PATHS * BLOCKS * ROWS, LANES)
    spectra = run_front(freqs, times, samples)
    return run_correlate(tile_map.shape[0] // times, tile_map, spectra)


def solution(mesh):
    in_specs = (P("freq", "tm", None, None), P())
    out_specs = P("tm", "freq", None, None, None)
    return jax.shard_map(
        on_device, mesh=mesh, in_specs=in_specs, out_specs=out_specs, check_vma=False
    )
```

```python
import functools
import itertools
import math

import jax
import jax.numpy as jnp
import numpy as np
from jax import lax
from jax.experimental import pallas as pl
from jax.experimental.pallas import tpu as pltpu
from jax.sharding import PartitionSpec as P

NCHAN = 4096
TAPS = 4
TB = 128
CHANNELS = 128
FIRST = NCHAN // 2 - CHANNELS // 2
CH_DEV = 2
LANES = 128
CHUNKS = NCHAN // LANES
ROWS = 2 * CHUNKS
PARTIAL = 16
FOLD = ROWS // PARTIAL
BLOCKS = 8
OUT = BLOCKS + TAPS - 1
PATHS = 16
SLOT = 16
SPECTRA = 32
QUADS = CHANNELS // 4
BATCH = 8
PIECES = 3
PARTS = 4
MESH = pl.DeviceIdType.MESH


def window_table():
    n = np.arange(TAPS * NCHAN, dtype=np.float64) + 0.5
    taper = 0.5 - 0.5 * np.cos(2.0 * math.pi * n / (TAPS * NCHAN))
    taps = np.sinc(n / NCHAN - TAPS / 2.0) * taper / (128.0 * math.sqrt(NCHAN))
    taps = np.repeat(taps.reshape(TAPS, CHUNKS, 1, LANES), 2, axis=2)
    return taps.reshape(TAPS, ROWS, LANES).astype(np.float32)


def turn_table():
    sample = np.arange(LANES)[:, None]
    m = np.arange(CHANNELS)[None, :]
    angle = (sample * (FIRST + m) % NCHAN) * (2.0 * math.pi / NCHAN)
    real, imag = np.cos(angle), -np.sin(angle)
    quarters = []
    for h in range(FOLD):
        turns = h * (NCHAN // FOLD) * (FIRST + m) % NCHAN // (NCHAN // FOLD)
        cosine, sine = (np.array(v)[turns] for v in ((1, 0, -1, 0), (0, -1, 0, 1)))
        quarters.append(
            np.concatenate(
                [real * cosine - imag * sine, real * sine + imag * cosine], axis=1
            )
        )
    return np.concatenate(quarters, axis=0).astype(np.float32).astype(jnp.bfloat16)


def run_table():
    run = np.arange(PARTIAL)[:, None] // 2
    part = np.arange(PARTIAL)[:, None] % 2
    m = np.arange(CHANNELS)[None, :]
    angle = (run * LANES * (FIRST + m) % NCHAN) * (2.0 * math.pi / NCHAN)
    turned = np.exp(-1j * angle) * np.where(part == 0, 1.0, 1j)
    return np.stack([turned.real, turned.imag]).astype(np.float32)


def quad_table():
    table = np.arange(QUADS)[:, None] == np.arange(CHANNELS)[None, :] // 4
    return table.astype(jnp.bfloat16)


def place_table(times):
    table = np.zeros((times, 2, 2, 2, SLOT, 2, 2, 2, SPECTRA), np.float32)
    for t in range(times):
        for step in range(OUT):
            if t * BLOCKS + step < times * BLOCKS:
                for e in range(2):
                    for c in range(2):
                        for q in range(2):
                            table[t, e, c, q, step, e, c, q, t * BLOCKS + step] = 1.0
    return table.reshape(times * LANES, 2 * LANES).astype(jnp.bfloat16)


def front(
    freqs,
    times,
    x_hbm,
    window_hbm,
    turn_hbm,
    runs_hbm,
    quads_hbm,
    place_hbm,
    spectra,
    x,
    window,
    turn,
    runs,
    quads,
    place,
    z,
    sums,
    mixed,
    packed,
    landed,
    ready,
    x_sem,
    table_sem,
    slice_send,
    slice_recv,
    spread_send,
    spread_recv,
    share_send,
    share_recv,
):
    f, t = lax.axis_index("freq"), lax.axis_index("tm")
    group = freqs // times
    rows = group * PATHS
    half = freqs // 2
    core, mine = f // half, lax.rem(t, 2)
    side, place_x = lax.rem(f, 2), t // 2
    among = (core == mine).astype(jnp.int32)

    def across(other):
        return jnp.where(other == side, place_x, 1 - place_x)
    per_path = BLOCKS * ROWS

    def fetch(i):
        at = pl.ds(pl.multiple_of(i * per_path, per_path), per_path)
        return pltpu.make_async_copy(x_hbm.at[at], x.at[at], x_sem.at[i])

    def start_fetch(i, carry):
        fetch(i).start()
        return carry

    tables = [
        pltpu.make_async_copy(source, target, table_sem.at[k])
        for k, (source, target) in enumerate(
            zip(
                (window_hbm, turn_hbm, runs_hbm, quads_hbm, place_hbm),
                (window, turn, runs, quads, place),
            )
        )
    ]
    tables[0].start()
    lax.fori_loop(0, BATCH, start_fetch, 0)
    for table in tables[1:4]:
        table.start()
    lax.fori_loop(BATCH, PATHS, start_fetch, 0)
    tables[4].start()

    barrier = pltpu.get_barrier_semaphore()
    for d in range(1, times):
        pl.semaphore_signal(
            barrier, inc=1, device_id=(f, lax.rem(t + d, times)), device_id_type=MESH
        )

    def greet(j, carry):
        source = half * mine + j
        time = 2 * across(lax.rem(source, 2)) + core

        @pl.when((source != f) | (time != t))
        def _():
            pl.semaphore_signal(
                barrier, inc=1, device_id=(source, time), device_id_type=MESH
            )

        return carry

    lax.fori_loop(0, half, greet, 0)
    sums[...] = jnp.zeros_like(sums)

    tables[0].wait()

    def channelize(n, carry):
        def filtered(path, carry):
            fetch(n * BATCH + path).wait()
            for h in range(FOLD):
                start = (n * BATCH + path) * per_path + h * PARTIAL
                taps = [
                    window[k, h * PARTIAL : (h + 1) * PARTIAL, :] for k in range(TAPS)
                ]
                steps = [
                    x[
                        pl.ds(pl.multiple_of(start + b * ROWS, PARTIAL), PARTIAL), :
                    ].astype(jnp.float32)
                    for b in range(BLOCKS)
                ]
                for s in range(OUT):
                    terms = [
                        taps[k] * steps[s - TAPS + 1 + k]
                        for k in range(TAPS)
                        if 0 <= s - TAPS + 1 + k < BLOCKS
                    ]
                    total = functools.reduce(lambda a, b: a + b, terms)
                    at = pl.multiple_of((path * OUT + s) * PARTIAL, PARTIAL)
                    z[pl.ds(at, PARTIAL), h * LANES : (h + 1) * LANES] = total.astype(
                        jnp.bfloat16
                    )
            return carry

        lax.fori_loop(0, BATCH, filtered, 0)

        @pl.when(n == 0)
        def _():
            for table in tables[1:3]:
                table.wait()

        u = jnp.dot(z[...], turn[...], preferred_element_type=jnp.float32)
        real, imag = runs[0], runs[1]
        for path in range(BATCH):
            at = pl.multiple_of((n * BATCH + path) * 2 * SLOT, 2 * SLOT)
            for s in range(OUT):
                k = (path * OUT + s) * PARTIAL
                u0, u1 = u[k : k + PARTIAL, :LANES], u[k : k + PARTIAL, LANES:]
                a = jnp.sum(real * u0 - imag * u1, axis=0, keepdims=True)
                b = jnp.sum(imag * u0 + real * u1, axis=0, keepdims=True)
                sums[pl.ds(at + s, 1), :] = a
                sums[pl.ds(at + SLOT + s, 1), :] = b
        return carry

    lax.fori_loop(0, PATHS // BATCH, channelize, 0)
    tables[3].wait()
    tables[4].wait()

    of_quad = lax.broadcasted_iota(jnp.int32, (2 * SLOT, LANES), 1) % 4
    for i in range(PATHS):
        value = sums[i * 2 * SLOT : (i + 1) * 2 * SLOT, :]
        four = jnp.concatenate(
            [jnp.where(of_quad == m, value, 0.0) for m in range(4)], axis=0
        ).astype(jnp.bfloat16)
        moved = lax.dot_general(
            quads[...],
            four,
            (((1,), (1,)), ((), ())),
            preferred_element_type=jnp.float32,
        )
        mixed[pl.ds(i, QUADS, stride=PATHS), :] = moved

    columns = group // 2
    z_here = lax.rem(f // 2, columns)
    far_first = [
        lax.rem(z_here + d, columns)
        for d in sorted(range(columns), key=lambda d: -min(d, columns - d))
    ]
    for to in range(times):
        for n, column in enumerate(far_first):
            at = pl.multiple_of((to * columns + column) * PATHS, PATHS)
            tile = mixed[pl.ds(at, PATHS), :]
            at = ((to // 2 * columns + n) * 2 + to % 2) * PATHS
            packed[at : at + PATHS, :] = tile.astype(jnp.bfloat16)

    pl.semaphore_wait(barrier, times - 1 + half - among)
    cuts = sorted({0, 1, columns // 2, columns})
    pieces = list(zip(cuts, cuts[1:]))
    slices = [[] for _ in pieces]
    for p, (low, high) in enumerate(pieces):
        size = (high - low) * 2 * PATHS
        for d in (2, 3, 1):
            to = t + d - 2 * (t & d)
            k = p * (times - 1) + d - 1
            at = lax.rem(to, 2) * rows + low * 2 * PATHS
            copy = pltpu.make_async_remote_copy(
                src_ref=packed.at[pl.ds(pl.multiple_of(at, PATHS), size)],
                dst_ref=landed.at[t, pl.ds(low * 2 * PATHS, size)],
                send_sem=slice_send.at[k],
                recv_sem=slice_recv.at[k],
                device_id=(f, to),
                device_id_type=MESH,
            )
            copy.start()
            slices[p].append(copy)
    landed[t] = packed[pl.ds(pl.multiple_of(mine * rows, rows), rows), :]

    here = spectra.at[pl.ds(pl.multiple_of(f * PATHS, PATHS), PATHS)]
    part = half // PARTS
    arrived = spread_recv.at[lax.rem(f // part, PARTS)]

    for p, (low, high) in enumerate(pieces):
        for copy in slices[p]:
            copy.wait_recv()
        piece = slice(low * 2 * PATHS, high * 2 * PATHS)
        joined = jnp.dot(
            jnp.concatenate([landed[j, piece, :] for j in range(times)], axis=1),
            place[...],
            preferred_element_type=jnp.float32,
        ).astype(jnp.bfloat16)
        for e in range(2):
            ready[e, piece, :] = joined[:, e * LANES : (e + 1) * LANES]
        for n, y, e in itertools.product(range(low, high), range(2), range(2)):
            to = (2 * mine + y) * group + far_first[n] * 2 + e
            time = 2 * across(e) + core
            tile = ready.at[e, pl.ds((n * 2 + y) * PATHS, PATHS)]
            copy = pltpu.make_async_remote_copy(
                src_ref=tile,
                dst_ref=here,
                send_sem=spread_send,
                recv_sem=arrived,
                device_id=(to, time),
                device_id_type=MESH,
            )
            if n < columns - 1:
                copy.start()
                continue
            local = (to == f) & (time == t)
            pl.when(jnp.logical_not(local))(copy.start)
            pl.when(local)(pltpu.make_async_copy(tile, here, arrived).start)

    mate = t + 1 - 2 * mine
    shared = []
    for k in range(PARTS):
        at = (mine * PARTS + k) * part * PATHS
        some = spectra.at[pl.ds(pl.multiple_of(at, part * PATHS), part * PATHS)]
        pltpu.make_async_copy(some, some, spread_recv.at[k]).wait()
        copy = pltpu.make_async_remote_copy(
            src_ref=some,
            dst_ref=some,
            send_sem=share_send.at[k],
            recv_sem=share_recv.at[k],
            device_id=(f, mate),
            device_id_type=MESH,
        )
        copy.start()
        shared.append(copy)
    for copy in sum(slices, []):
        copy.wait_send()

    def drain(count):
        some = spectra.at[pl.ds(0, count * PATHS)]
        pltpu.make_async_copy(some, some, spread_send).wait()

    @pl.when(among == 1)
    def _():
        drain(half - 1)

    @pl.when(among == 0)
    def _():
        drain(half)

    for copy in shared:
        copy.wait()


def correlate(slots, ids, spectra, out, tiles, sems):
    t = lax.axis_index("tm")
    lane = lax.broadcasted_iota(jnp.int32, (TB, LANES), 1)
    first = lane < LANES // 2
    even = lane // SPECTRA % 2 == 0
    for j in range(slots):
        number = ids[t * slots + j]
        row = jnp.int32(0)
        for k in range(1, 8):
            row = row + (number >= k * (k + 1) // 2).astype(jnp.int32)
        col = number - row * (row + 1) // 2
        left = spectra[pl.ds(pl.multiple_of(row * TB, TB), TB), :].astype(jnp.float32)
        right = spectra[pl.ds(pl.multiple_of(col * TB, TB), TB), :]
        turned = jnp.where(
            even,
            pltpu.roll(left, LANES - SPECTRA, 1),
            -pltpu.roll(left, SPECTRA, 1),
        )
        four = jnp.concatenate(
            [
                jnp.where(first, left, 0.0),
                jnp.where(first, turned, 0.0),
                jnp.where(first, 0.0, left),
                jnp.where(first, 0.0, turned),
            ],
            axis=0,
        ).astype(jnp.bfloat16)
        products = lax.dot_general(
            four, right, (((1,), (1,)), ((), ())), preferred_element_type=jnp.float32
        )
        tiles[j] = (products * (1.0 / SPECTRA)).reshape(CH_DEV, 2, TB, TB)
        pltpu.make_async_copy(tiles.at[j], out.at[j], sems.at[j]).start()
    for j in range(slots):
        pltpu.make_async_copy(tiles.at[j], out.at[j], sems.at[j]).wait()


def run_front(freqs, times, samples):
    rows = freqs // times * PATHS
    dma = pltpu.SemaphoreType.DMA
    hbm = pl.BlockSpec(memory_space=pl.ANY)
    tables = [
        window_table(),
        turn_table(),
        run_table(),
        quad_table(),
        place_table(times),
    ]
    return pl.pallas_call(
        functools.partial(front, freqs, times),
        out_shape=pltpu.VMEM((freqs * PATHS, LANES), jnp.bfloat16),
        in_specs=[hbm] * (1 + len(tables)),
        out_specs=hbm,
        scratch_shapes=[
            pltpu.VMEM((PATHS * BLOCKS * ROWS, LANES), jnp.int32),
            *[pltpu.VMEM(table.shape, table.dtype) for table in tables],
            pltpu.VMEM((BATCH * OUT * PARTIAL, FOLD * LANES), jnp.bfloat16),
            pltpu.VMEM((PATHS * 2 * SLOT, LANES), jnp.float32),
            pltpu.VMEM((QUADS * PATHS, LANES), jnp.float32),
            pltpu.VMEM((QUADS * PATHS, LANES), jnp.bfloat16),
            pltpu.VMEM((times, rows, LANES), jnp.bfloat16),
            pltpu.VMEM((2, rows, LANES), jnp.bfloat16),
            dma((PATHS,)),
            dma((len(tables),)),
            dma((PIECES * (times - 1),)),
            dma((PIECES * (times - 1),)),
            dma,
            dma((PARTS,)),
            dma((PARTS,)),
            dma((PARTS,)),
        ],
        compiler_params=pltpu.CompilerParams(
            collective_id=0, has_side_effects=True, vmem_limit_bytes=60 * 2**20
        ),
        name="front",
    )(samples, *[jnp.asarray(table) for table in tables])


def run_correlate(slots, tile_map, spectra):
    return pl.pallas_call(
        functools.partial(correlate, slots),
        out_shape=jax.ShapeDtypeStruct((slots, CH_DEV, 2, TB, TB), jnp.float32),
        in_specs=[
            pl.BlockSpec(memory_space=pltpu.SMEM),
            pl.BlockSpec(memory_space=pltpu.VMEM),
        ],
        out_specs=pl.BlockSpec(memory_space=pl.ANY),
        scratch_shapes=[
            pltpu.VMEM((slots, CH_DEV, 2, TB, TB), jnp.float32),
            pltpu.SemaphoreType.DMA((slots,)),
        ],
        compiler_params=pltpu.CompilerParams(vmem_limit_bytes=40 * 2**20),
        name="correlate",
    )(tile_map, spectra)


def on_device(voltages, tile_map):
    freqs, times = lax.axis_size("freq"), lax.axis_size("tm")
    samples = voltages.reshape(PATHS, BLOCKS, 2, CHUNKS, LANES)
    samples = samples.transpose(0, 1, 3, 2, 4).reshape(PATHS * BLOCKS * ROWS, LANES)
    spectra = run_front(freqs, times, samples)
    return run_correlate(tile_map.shape[0] // times, tile_map, spectra)


def solution(mesh):
    in_specs = (P("freq", "tm", None, None), P())
    out_specs = P("tm", "freq", None, None, None)
    return jax.shard_map(
        on_device, mesh=mesh, in_specs=in_specs, out_specs=out_specs, check_vma=False
    )
```

```python
import functools
import itertools
import math

import jax
import jax.numpy as jnp
import numpy as np
from jax import lax
from jax.experimental import pallas as pl
from jax.experimental.pallas import tpu as pltpu
from jax.sharding import PartitionSpec as P

NCHAN = 4096
TAPS = 4
TB = 128
CHANNELS = 128
FIRST = NCHAN // 2 - CHANNELS // 2
CH_DEV = 2
LANES = 128
CHUNKS = NCHAN // LANES
ROWS = 2 * CHUNKS
PARTIAL = 16
FOLD = ROWS // PARTIAL
BLOCKS = 8
OUT = BLOCKS + TAPS - 1
PATHS = 16
SLOT = 16
SPECTRA = 32
QUADS = CHANNELS // 4
BATCH = 8
PIECES = 3
PARTS = 4
MESH = pl.DeviceIdType.MESH


def window_table():
    n = np.arange(TAPS * NCHAN, dtype=np.float64) + 0.5
    taper = 0.5 - 0.5 * np.cos(2.0 * math.pi * n / (TAPS * NCHAN))
    taps = np.sinc(n / NCHAN - TAPS / 2.0) * taper / (128.0 * math.sqrt(NCHAN))
    taps = np.repeat(taps.reshape(TAPS, CHUNKS, 1, LANES), 2, axis=2)
    return taps.reshape(TAPS, ROWS, LANES).astype(np.float32)


def turn_table():
    sample = np.arange(LANES)[:, None]
    m = np.arange(CHANNELS)[None, :]
    angle = (sample * (FIRST + m) % NCHAN) * (2.0 * math.pi / NCHAN)
    real, imag = np.cos(angle), -np.sin(angle)
    quarters = []
    for h in range(FOLD):
        turns = h * (NCHAN // FOLD) * (FIRST + m) % NCHAN // (NCHAN // FOLD)
        cosine, sine = (np.array(v)[turns] for v in ((1, 0, -1, 0), (0, -1, 0, 1)))
        quarters.append(
            np.concatenate(
                [real * cosine - imag * sine, real * sine + imag * cosine], axis=1
            )
        )
    return np.concatenate(quarters, axis=0).astype(np.float32).astype(jnp.bfloat16)


def run_table():
    run = np.arange(PARTIAL)[:, None] // 2
    part = np.arange(PARTIAL)[:, None] % 2
    m = np.arange(CHANNELS)[None, :]
    angle = (run * LANES * (FIRST + m) % NCHAN) * (2.0 * math.pi / NCHAN)
    turned = np.exp(-1j * angle) * np.where(part == 0, 1.0, 1j)
    return np.stack([turned.real, turned.imag]).astype(np.float32)


def quad_table():
    table = np.arange(QUADS)[:, None] == np.arange(CHANNELS)[None, :] // 4
    return table.astype(jnp.bfloat16)


def place_table(times):
    table = np.zeros((times, 2, 2, 2, SLOT, 2, 2, 2, SPECTRA), np.float32)
    for t in range(times):
        for step in range(OUT):
            if t * BLOCKS + step < times * BLOCKS:
                for e in range(2):
                    for c in range(2):
                        for q in range(2):
                            table[t, e, c, q, step, e, c, q, t * BLOCKS + step] = 1.0
    return table.reshape(times * LANES, 2 * LANES).astype(jnp.bfloat16)


def front(
    freqs,
    times,
    x_hbm,
    window_hbm,
    turn_hbm,
    runs_hbm,
    quads_hbm,
    place_hbm,
    spectra,
    x,
    window,
    turn,
    runs,
    quads,
    place,
    z,
    sums,
    mixed,
    packed,
    landed,
    ready,
    x_sem,
    table_sem,
    slice_send,
    slice_recv,
    spread_send,
    spread_recv,
    share_send,
    share_recv,
):
    f, t = lax.axis_index("freq"), lax.axis_index("tm")
    group = freqs // times
    rows = group * PATHS
    half = freqs // 2
    core, mine = f // half, lax.rem(t, 2)
    side, place_x = lax.rem(f, 2), t // 2
    among = (core == mine).astype(jnp.int32)

    def across(other):
        return jnp.where(other == side, place_x, 1 - place_x)
    per_path = BLOCKS * ROWS

    def fetch(i):
        at = pl.ds(pl.multiple_of(i * per_path, per_path), per_path)
        return pltpu.make_async_copy(x_hbm.at[at], x.at[at], x_sem.at[i])

    def start_fetch(i, carry):
        fetch(i).start()
        return carry

    tables = [
        pltpu.make_async_copy(source, target, table_sem.at[k])
        for k, (source, target) in enumerate(
            zip(
                (window_hbm, turn_hbm, runs_hbm, quads_hbm, place_hbm),
                (window, turn, runs, quads, place),
            )
        )
    ]
    tables[0].start()
    lax.fori_loop(0, BATCH, start_fetch, 0)
    columns = group // 2
    z_here = lax.rem(f // 2, columns)
    far_first = [
        lax.rem(z_here + d, columns)
        for d in sorted(range(columns), key=lambda d: -min(d, columns - d))
    ]

    barrier = pltpu.get_barrier_semaphore()
    for n, y, e in itertools.product(range(columns), range(2), range(2)):
        source = (2 * mine + y) * group + far_first[n] * 2 + e
        time = 2 * across(e) + core
        greet = functools.partial(
            pl.semaphore_signal,
            barrier,
            inc=1,
            device_id=(source, time),
            device_id_type=MESH,
        )
        if n < columns - 1:
            greet()
        else:
            pl.when((source != f) | (time != t))(greet)
    for d in range(1, times):
        pl.semaphore_signal(
            barrier, inc=1, device_id=(f, lax.rem(t + d, times)), device_id_type=MESH
        )
    for table in tables[1:4]:
        table.start()
    lax.fori_loop(BATCH, PATHS, start_fetch, 0)
    tables[4].start()

    sums[...] = jnp.zeros_like(sums)

    tables[0].wait()

    def channelize(n, carry):
        def filtered(path, carry):
            fetch(n * BATCH + path).wait()
            for h in range(FOLD):
                start = (n * BATCH + path) * per_path + h * PARTIAL
                taps = [
                    window[k, h * PARTIAL : (h + 1) * PARTIAL, :] for k in range(TAPS)
                ]
                steps = [
                    x[
                        pl.ds(pl.multiple_of(start + b * ROWS, PARTIAL), PARTIAL), :
                    ].astype(jnp.float32)
                    for b in range(BLOCKS)
                ]
                for s in range(OUT):
                    terms = [
                        taps[k] * steps[s - TAPS + 1 + k]
                        for k in range(TAPS)
                        if 0 <= s - TAPS + 1 + k < BLOCKS
                    ]
                    total = functools.reduce(lambda a, b: a + b, terms)
                    at = pl.multiple_of((path * OUT + s) * PARTIAL, PARTIAL)
                    z[pl.ds(at, PARTIAL), h * LANES : (h + 1) * LANES] = total.astype(
                        jnp.bfloat16
                    )
            return carry

        lax.fori_loop(0, BATCH, filtered, 0)

        @pl.when(n == 0)
        def _():
            for table in tables[1:3]:
                table.wait()

        u = jnp.dot(z[...], turn[...], preferred_element_type=jnp.float32)
        real, imag = runs[0], runs[1]
        for path in range(BATCH):
            at = pl.multiple_of((n * BATCH + path) * 2 * SLOT, 2 * SLOT)
            for s in range(OUT):
                k = (path * OUT + s) * PARTIAL
                u0, u1 = u[k : k + PARTIAL, :LANES], u[k : k + PARTIAL, LANES:]
                a = jnp.sum(real * u0 - imag * u1, axis=0, keepdims=True)
                b = jnp.sum(imag * u0 + real * u1, axis=0, keepdims=True)
                sums[pl.ds(at + s, 1), :] = a
                sums[pl.ds(at + SLOT + s, 1), :] = b
        return carry

    lax.fori_loop(0, PATHS // BATCH, channelize, 0)
    tables[3].wait()
    tables[4].wait()

    of_quad = lax.broadcasted_iota(jnp.int32, (2 * SLOT, LANES), 1) % 4
    for i in range(PATHS):
        value = sums[i * 2 * SLOT : (i + 1) * 2 * SLOT, :]
        four = jnp.concatenate(
            [jnp.where(of_quad == m, value, 0.0) for m in range(4)], axis=0
        ).astype(jnp.bfloat16)
        moved = lax.dot_general(
            quads[...],
            four,
            (((1,), (1,)), ((), ())),
            preferred_element_type=jnp.float32,
        )
        mixed[pl.ds(i, QUADS, stride=PATHS), :] = moved

    for to in range(times):
        for n, column in enumerate(far_first):
            at = pl.multiple_of((to * columns + column) * PATHS, PATHS)
            tile = mixed[pl.ds(at, PATHS), :]
            at = ((to // 2 * columns + n) * 2 + to % 2) * PATHS
            packed[at : at + PATHS, :] = tile.astype(jnp.bfloat16)

    pl.semaphore_wait(barrier, times - 1 + half - among)
    cuts = sorted({0, 1, columns // 2, columns})
    pieces = list(zip(cuts, cuts[1:]))
    slices = [[] for _ in pieces]
    for p, (low, high) in enumerate(pieces):
        size = (high - low) * 2 * PATHS
        for d in (2, 3, 1):
            to = t + d - 2 * (t & d)
            k = p * (times - 1) + d - 1
            at = lax.rem(to, 2) * rows + low * 2 * PATHS
            copy = pltpu.make_async_remote_copy(
                src_ref=packed.at[pl.ds(pl.multiple_of(at, PATHS), size)],
                dst_ref=landed.at[t, pl.ds(low * 2 * PATHS, size)],
                send_sem=slice_send.at[k],
                recv_sem=slice_recv.at[k],
                device_id=(f, to),
                device_id_type=MESH,
            )
            copy.start()
            slices[p].append(copy)
    landed[t] = packed[pl.ds(pl.multiple_of(mine * rows, rows), rows), :]

    here = spectra.at[pl.ds(pl.multiple_of(f * PATHS, PATHS), PATHS)]
    part = half // PARTS
    arrived = spread_recv.at[lax.rem(f // part, PARTS)]

    for p, (low, high) in enumerate(pieces):
        for copy in slices[p]:
            copy.wait_recv()
        piece = slice(low * 2 * PATHS, high * 2 * PATHS)
        joined = jnp.dot(
            jnp.concatenate([landed[j, piece, :] for j in range(times)], axis=1),
            place[...],
            preferred_element_type=jnp.float32,
        ).astype(jnp.bfloat16)
        for e in range(2):
            ready[e, piece, :] = joined[:, e * LANES : (e + 1) * LANES]
        for n, y, e in itertools.product(range(low, high), range(2), range(2)):
            to = (2 * mine + y) * group + far_first[n] * 2 + e
            time = 2 * across(e) + core
            tile = ready.at[e, pl.ds((n * 2 + y) * PATHS, PATHS)]
            copy = pltpu.make_async_remote_copy(
                src_ref=tile,
                dst_ref=here,
                send_sem=spread_send,
                recv_sem=arrived,
                device_id=(to, time),
                device_id_type=MESH,
            )
            if n < columns - 1:
                copy.start()
                continue
            local = (to == f) & (time == t)
            pl.when(jnp.logical_not(local))(copy.start)
            pl.when(local)(pltpu.make_async_copy(tile, here, arrived).start)

    mate = t + 1 - 2 * mine
    shared = []
    for k in range(PARTS):
        at = (mine * PARTS + k) * part * PATHS
        some = spectra.at[pl.ds(pl.multiple_of(at, part * PATHS), part * PATHS)]
        pltpu.make_async_copy(some, some, spread_recv.at[k]).wait()
        copy = pltpu.make_async_remote_copy(
            src_ref=some,
            dst_ref=some,
            send_sem=share_send.at[k],
            recv_sem=share_recv.at[k],
            device_id=(f, mate),
            device_id_type=MESH,
        )
        copy.start()
        shared.append(copy)
    for copy in sum(slices, []):
        copy.wait_send()

    def drain(count):
        some = spectra.at[pl.ds(0, count * PATHS)]
        pltpu.make_async_copy(some, some, spread_send).wait()

    @pl.when(among == 1)
    def _():
        drain(half - 1)

    @pl.when(among == 0)
    def _():
        drain(half)

    for copy in shared:
        copy.wait()


def correlate(slots, ids, spectra, out, tiles, sems):
    t = lax.axis_index("tm")
    lane = lax.broadcasted_iota(jnp.int32, (TB, LANES), 1)
    first = lane < LANES // 2
    even = lane // SPECTRA % 2 == 0
    for j in range(slots):
        number = ids[t * slots + j]
        row = jnp.int32(0)
        for k in range(1, 8):
            row = row + (number >= k * (k + 1) // 2).astype(jnp.int32)
        col = number - row * (row + 1) // 2
        left = spectra[pl.ds(pl.multiple_of(row * TB, TB), TB), :].astype(jnp.float32)
        right = spectra[pl.ds(pl.multiple_of(col * TB, TB), TB), :]
        turned = jnp.where(
            even,
            pltpu.roll(left, LANES - SPECTRA, 1),
            -pltpu.roll(left, SPECTRA, 1),
        )
        four = jnp.concatenate(
            [
                jnp.where(first, left, 0.0),
                jnp.where(first, turned, 0.0),
                jnp.where(first, 0.0, left),
                jnp.where(first, 0.0, turned),
            ],
            axis=0,
        ).astype(jnp.bfloat16)
        products = lax.dot_general(
            four, right, (((1,), (1,)), ((), ())), preferred_element_type=jnp.float32
        )
        tiles[j] = (products * (1.0 / SPECTRA)).reshape(CH_DEV, 2, TB, TB)
        pltpu.make_async_copy(tiles.at[j], out.at[j], sems.at[j]).start()
    for j in range(slots):
        pltpu.make_async_copy(tiles.at[j], out.at[j], sems.at[j]).wait()


def run_front(freqs, times, samples):
    rows = freqs // times * PATHS
    dma = pltpu.SemaphoreType.DMA
    hbm = pl.BlockSpec(memory_space=pl.ANY)
    tables = [
        window_table(),
        turn_table(),
        run_table(),
        quad_table(),
        place_table(times),
    ]
    return pl.pallas_call(
        functools.partial(front, freqs, times),
        out_shape=pltpu.VMEM((freqs * PATHS, LANES), jnp.bfloat16),
        in_specs=[hbm] * (1 + len(tables)),
        out_specs=hbm,
        scratch_shapes=[
            pltpu.VMEM((PATHS * BLOCKS * ROWS, LANES), jnp.int32),
            *[pltpu.VMEM(table.shape, table.dtype) for table in tables],
            pltpu.VMEM((BATCH * OUT * PARTIAL, FOLD * LANES), jnp.bfloat16),
            pltpu.VMEM((PATHS * 2 * SLOT, LANES), jnp.float32),
            pltpu.VMEM((QUADS * PATHS, LANES), jnp.float32),
            pltpu.VMEM((QUADS * PATHS, LANES), jnp.bfloat16),
            pltpu.VMEM((times, rows, LANES), jnp.bfloat16),
            pltpu.VMEM((2, rows, LANES), jnp.bfloat16),
            dma((PATHS,)),
            dma((len(tables),)),
            dma((PIECES * (times - 1),)),
            dma((PIECES * (times - 1),)),
            dma,
            dma((PARTS,)),
            dma((PARTS,)),
            dma((PARTS,)),
        ],
        compiler_params=pltpu.CompilerParams(
            collective_id=0, has_side_effects=True, vmem_limit_bytes=60 * 2**20
        ),
        name="front",
    )(samples, *[jnp.asarray(table) for table in tables])


def run_correlate(slots, tile_map, spectra):
    return pl.pallas_call(
        functools.partial(correlate, slots),
        out_shape=jax.ShapeDtypeStruct((slots, CH_DEV, 2, TB, TB), jnp.float32),
        in_specs=[
            pl.BlockSpec(memory_space=pltpu.SMEM),
            pl.BlockSpec(memory_space=pltpu.VMEM),
        ],
        out_specs=pl.BlockSpec(memory_space=pl.ANY),
        scratch_shapes=[
            pltpu.VMEM((slots, CH_DEV, 2, TB, TB), jnp.float32),
            pltpu.SemaphoreType.DMA((slots,)),
        ],
        compiler_params=pltpu.CompilerParams(vmem_limit_bytes=40 * 2**20),
        name="correlate",
    )(tile_map, spectra)


def on_device(voltages, tile_map):
    freqs, times = lax.axis_size("freq"), lax.axis_size("tm")
    samples = voltages.reshape(PATHS, BLOCKS, 2, CHUNKS, LANES)
    samples = samples.transpose(0, 1, 3, 2, 4).reshape(PATHS * BLOCKS * ROWS, LANES)
    spectra = run_front(freqs, times, samples)
    return run_correlate(tile_map.shape[0] // times, tile_map, spectra)


def solution(mesh):
    in_specs = (P("freq", "tm", None, None), P())
    out_specs = P("tm", "freq", None, None, None)
    return jax.shard_map(
        on_device, mesh=mesh, in_specs=in_specs, out_specs=out_specs, check_vma=False
    )
```

```python
import functools
import itertools
import math

import jax
import jax.numpy as jnp
import numpy as np
from jax import lax
from jax.experimental import pallas as pl
from jax.experimental.pallas import tpu as pltpu
from jax.sharding import PartitionSpec as P

NCHAN = 4096
TAPS = 4
TB = 128
CHANNELS = 128
FIRST = NCHAN // 2 - CHANNELS // 2
CH_DEV = 2
LANES = 128
CHUNKS = NCHAN // LANES
ROWS = 2 * CHUNKS
PARTIAL = 16
FOLD = ROWS // PARTIAL
BLOCKS = 8
OUT = BLOCKS + TAPS - 1
PATHS = 16
SLOT = 16
SPECTRA = 32
QUADS = CHANNELS // 4
BATCH = 8
PIECES = 3
PARTS = 4
MESH = pl.DeviceIdType.MESH


def window_table():
    n = np.arange(TAPS * NCHAN, dtype=np.float64) + 0.5
    taper = 0.5 - 0.5 * np.cos(2.0 * math.pi * n / (TAPS * NCHAN))
    taps = np.sinc(n / NCHAN - TAPS / 2.0) * taper / (128.0 * math.sqrt(NCHAN))
    taps = np.repeat(taps.reshape(TAPS, CHUNKS, 1, LANES), 2, axis=2)
    return taps.reshape(TAPS, ROWS, LANES).astype(np.float32)


def turn_table():
    sample = np.arange(LANES)[:, None]
    m = np.arange(CHANNELS)[None, :]
    angle = (sample * (FIRST + m) % NCHAN) * (2.0 * math.pi / NCHAN)
    real, imag = np.cos(angle), -np.sin(angle)
    quarters = []
    for h in range(FOLD):
        turns = h * (NCHAN // FOLD) * (FIRST + m) % NCHAN // (NCHAN // FOLD)
        cosine, sine = (np.array(v)[turns] for v in ((1, 0, -1, 0), (0, -1, 0, 1)))
        quarters.append(
            np.concatenate(
                [real * cosine - imag * sine, real * sine + imag * cosine], axis=1
            )
        )
    return np.concatenate(quarters, axis=0).astype(np.float32).astype(jnp.bfloat16)


def run_table():
    run = np.arange(PARTIAL)[:, None] // 2
    part = np.arange(PARTIAL)[:, None] % 2
    m = np.arange(CHANNELS)[None, :]
    angle = (run * LANES * (FIRST + m) % NCHAN) * (2.0 * math.pi / NCHAN)
    turned = np.exp(-1j * angle) * np.where(part == 0, 1.0, 1j)
    return np.stack([turned.real, turned.imag]).astype(np.float32)


def quad_table():
    table = np.arange(QUADS)[:, None] == np.arange(CHANNELS)[None, :] // 4
    return table.astype(jnp.bfloat16)


def place_table(times):
    table = np.zeros((times, 2, 2, 2, SLOT, 2, 2, 2, SPECTRA), np.float32)
    for t in range(times):
        for step in range(OUT):
            if t * BLOCKS + step < times * BLOCKS:
                for e in range(2):
                    for c in range(2):
                        for q in range(2):
                            table[t, e, c, q, step, e, c, q, t * BLOCKS + step] = 1.0
    return table.reshape(times * LANES, 2 * LANES).astype(jnp.bfloat16)


def front(
    freqs,
    times,
    x_hbm,
    window_hbm,
    turn_hbm,
    runs_hbm,
    quads_hbm,
    place_hbm,
    spectra,
    x,
    window,
    turn,
    runs,
    quads,
    place,
    z,
    sums,
    mixed,
    packed,
    landed,
    ready,
    x_sem,
    table_sem,
    slice_send,
    slice_recv,
    spread_send,
    spread_recv,
    share_send,
    share_recv,
):
    f, t = lax.axis_index("freq"), lax.axis_index("tm")
    group = freqs // times
    rows = group * PATHS
    half = freqs // 2
    core, mine = f // half, lax.rem(t, 2)
    side, place_x = lax.rem(f, 2), t // 2
    among = (core == mine).astype(jnp.int32)

    def across(other):
        return jnp.where(other == side, place_x, 1 - place_x)
    per_path = BLOCKS * ROWS

    def fetch(i):
        at = pl.ds(pl.multiple_of(i * per_path, per_path), per_path)
        return pltpu.make_async_copy(x_hbm.at[at], x.at[at], x_sem.at[i])

    def start_fetch(i, carry):
        fetch(i).start()
        return carry

    tables = [
        pltpu.make_async_copy(source, target, table_sem.at[k])
        for k, (source, target) in enumerate(
            zip(
                (window_hbm, turn_hbm, runs_hbm, quads_hbm, place_hbm),
                (window, turn, runs, quads, place),
            )
        )
    ]
    tables[0].start()
    lax.fori_loop(0, BATCH, start_fetch, 0)
    columns = group // 2
    z_here = lax.rem(f // 2, columns)
    far_first = [
        lax.rem(z_here + d, columns)
        for d in sorted(range(columns), key=lambda d: -min(d, columns - d))
    ]

    barrier = pltpu.get_barrier_semaphore()
    for n, y, e in itertools.product(range(columns), range(2), range(2)):
        source = (2 * mine + y) * group + far_first[n] * 2 + e
        time = 2 * across(e) + core
        greet = functools.partial(
            pl.semaphore_signal,
            barrier,
            inc=1,
            device_id=(source, time),
            device_id_type=MESH,
        )
        if n < columns - 1:
            greet()
        else:
            pl.when((source != f) | (time != t))(greet)
    for d in range(1, times):
        pl.semaphore_signal(
            barrier, inc=1, device_id=(f, lax.rem(t + d, times)), device_id_type=MESH
        )
    for table in tables[1:4]:
        table.start()
    lax.fori_loop(BATCH, PATHS, start_fetch, 0)
    tables[4].start()

    sums[...] = jnp.zeros_like(sums)

    tables[0].wait()

    def channelize(n, carry):
        def filtered(path, carry):
            fetch(n * BATCH + path).wait()
            for h in range(FOLD):
                start = (n * BATCH + path) * per_path + h * PARTIAL
                taps = [
                    window[k, h * PARTIAL : (h + 1) * PARTIAL, :] for k in range(TAPS)
                ]
                steps = [
                    x[
                        pl.ds(pl.multiple_of(start + b * ROWS, PARTIAL), PARTIAL), :
                    ].astype(jnp.float32)
                    for b in range(BLOCKS)
                ]
                for s in range(OUT):
                    terms = [
                        taps[k] * steps[s - TAPS + 1 + k]
                        for k in range(TAPS)
                        if 0 <= s - TAPS + 1 + k < BLOCKS
                    ]
                    total = functools.reduce(lambda a, b: a + b, terms)
                    at = pl.multiple_of((path * OUT + s) * PARTIAL, PARTIAL)
                    z[pl.ds(at, PARTIAL), h * LANES : (h + 1) * LANES] = total.astype(
                        jnp.bfloat16
                    )
            return carry

        lax.fori_loop(0, BATCH, filtered, 0)

        @pl.when(n == 0)
        def _():
            for table in tables[1:3]:
                table.wait()

        u = jnp.dot(z[...], turn[...], preferred_element_type=jnp.float32)
        real, imag = runs[0], runs[1]
        for path in range(BATCH):
            at = pl.multiple_of((n * BATCH + path) * 2 * SLOT, 2 * SLOT)
            for s in range(OUT):
                k = (path * OUT + s) * PARTIAL
                u0, u1 = u[k : k + PARTIAL, :LANES], u[k : k + PARTIAL, LANES:]
                a = jnp.sum(real * u0 - imag * u1, axis=0, keepdims=True)
                b = jnp.sum(imag * u0 + real * u1, axis=0, keepdims=True)
                sums[pl.ds(at + s, 1), :] = a
                sums[pl.ds(at + SLOT + s, 1), :] = b
        return carry

    lax.fori_loop(0, PATHS // BATCH, channelize, 0)
    tables[3].wait()
    tables[4].wait()

    of_quad = lax.broadcasted_iota(jnp.int32, (2 * SLOT, LANES), 1) % 4
    for i in range(PATHS):
        value = sums[i * 2 * SLOT : (i + 1) * 2 * SLOT, :]
        four = jnp.concatenate(
            [jnp.where(of_quad == m, value, 0.0) for m in range(4)], axis=0
        ).astype(jnp.bfloat16)
        moved = lax.dot_general(
            quads[...],
            four,
            (((1,), (1,)), ((), ())),
            preferred_element_type=jnp.float32,
        )
        mixed[pl.ds(i, QUADS, stride=PATHS), :] = moved

    for to in range(times):
        for n, column in enumerate(far_first):
            at = pl.multiple_of((to * columns + column) * PATHS, PATHS)
            tile = mixed[pl.ds(at, PATHS), :]
            at = ((to // 2 * columns + n) * 2 + to % 2) * PATHS
            packed[at : at + PATHS, :] = tile.astype(jnp.bfloat16)

    pl.semaphore_wait(barrier, times - 1 + half - among)
    cuts = sorted({0, 1, columns // 2, columns})
    pieces = list(zip(cuts, cuts[1:]))
    slices = [[] for _ in pieces]
    for p, (low, high) in enumerate(pieces):
        size = (high - low) * 2 * PATHS
        for d in (2, 3, 1):
            to = t + d - 2 * (t & d)
            k = p * (times - 1) + d - 1
            at = lax.rem(to, 2) * rows + low * 2 * PATHS
            copy = pltpu.make_async_remote_copy(
                src_ref=packed.at[pl.ds(pl.multiple_of(at, PATHS), size)],
                dst_ref=landed.at[t, pl.ds(low * 2 * PATHS, size)],
                send_sem=slice_send.at[k],
                recv_sem=slice_recv.at[k],
                device_id=(f, to),
                device_id_type=MESH,
            )
            copy.start()
            slices[p].append(copy)
    landed[t] = packed[pl.ds(pl.multiple_of(mine * rows, rows), rows), :]

    here = spectra.at[pl.ds(pl.multiple_of(f * PATHS, PATHS), PATHS)]
    part = half // PARTS
    arrived = spread_recv.at[lax.rem(f // part, PARTS)]

    for p, (low, high) in enumerate(pieces):
        for copy in slices[p]:
            copy.wait_recv()
        piece = slice(low * 2 * PATHS, high * 2 * PATHS)
        joined = jnp.dot(
            jnp.concatenate([landed[j, piece, :] for j in range(times)], axis=1),
            place[...],
            preferred_element_type=jnp.float32,
        ).astype(jnp.bfloat16)
        for e in range(2):
            ready[e, piece, :] = joined[:, e * LANES : (e + 1) * LANES]
        for n, y, e in itertools.product(range(low, high), range(2), range(2)):
            to = (2 * mine + y) * group + far_first[n] * 2 + e
            time = 2 * across(e) + core
            tile = ready.at[e, pl.ds((n * 2 + y) * PATHS, PATHS)]
            copy = pltpu.make_async_remote_copy(
                src_ref=tile,
                dst_ref=here,
                send_sem=spread_send,
                recv_sem=arrived,
                device_id=(to, time),
                device_id_type=MESH,
            )
            if n < columns - 1:
                copy.start()
                continue
            local = (to == f) & (time == t)
            pl.when(jnp.logical_not(local))(copy.start)
            pl.when(local)(pltpu.make_async_copy(tile, here, arrived).start)

    mate = t + 1 - 2 * mine
    shared = []
    near = z_here // max(columns // 2, 1)
    for n in range(PARTS):
        k = n % 2 * 2 + (near if n < 2 else 1 - near)
        at = (mine * PARTS + k) * part * PATHS
        some = spectra.at[pl.ds(pl.multiple_of(at, part * PATHS), part * PATHS)]
        pltpu.make_async_copy(some, some, spread_recv.at[k]).wait()
        copy = pltpu.make_async_remote_copy(
            src_ref=some,
            dst_ref=some,
            send_sem=share_send.at[k],
            recv_sem=share_recv.at[k],
            device_id=(f, mate),
            device_id_type=MESH,
        )
        copy.start()
        shared.append(copy)
    for copy in sum(slices, []):
        copy.wait_send()

    def drain(count):
        some = spectra.at[pl.ds(0, count * PATHS)]
        pltpu.make_async_copy(some, some, spread_send).wait()

    @pl.when(among == 1)
    def _():
        drain(half - 1)

    @pl.when(among == 0)
    def _():
        drain(half)

    for copy in shared:
        copy.wait()


def correlate(slots, ids, spectra, out, tiles, sems):
    t = lax.axis_index("tm")
    lane = lax.broadcasted_iota(jnp.int32, (TB, LANES), 1)
    first = lane < LANES // 2
    even = lane // SPECTRA % 2 == 0
    for j in range(slots):
        number = ids[t * slots + j]
        row = jnp.int32(0)
        for k in range(1, 8):
            row = row + (number >= k * (k + 1) // 2).astype(jnp.int32)
        col = number - row * (row + 1) // 2
        left = spectra[pl.ds(pl.multiple_of(row * TB, TB), TB), :].astype(jnp.float32)
        right = spectra[pl.ds(pl.multiple_of(col * TB, TB), TB), :]
        turned = jnp.where(
            even,
            pltpu.roll(left, LANES - SPECTRA, 1),
            -pltpu.roll(left, SPECTRA, 1),
        )
        four = jnp.concatenate(
            [
                jnp.where(first, left, 0.0),
                jnp.where(first, turned, 0.0),
                jnp.where(first, 0.0, left),
                jnp.where(first, 0.0, turned),
            ],
            axis=0,
        ).astype(jnp.bfloat16)
        products = lax.dot_general(
            four, right, (((1,), (1,)), ((), ())), preferred_element_type=jnp.float32
        )
        tiles[j] = (products * (1.0 / SPECTRA)).reshape(CH_DEV, 2, TB, TB)
        pltpu.make_async_copy(tiles.at[j], out.at[j], sems.at[j]).start()
    for j in range(slots):
        pltpu.make_async_copy(tiles.at[j], out.at[j], sems.at[j]).wait()


def run_front(freqs, times, samples):
    rows = freqs // times * PATHS
    dma = pltpu.SemaphoreType.DMA
    hbm = pl.BlockSpec(memory_space=pl.ANY)
    tables = [
        window_table(),
        turn_table(),
        run_table(),
        quad_table(),
        place_table(times),
    ]
    return pl.pallas_call(
        functools.partial(front, freqs, times),
        out_shape=pltpu.VMEM((freqs * PATHS, LANES), jnp.bfloat16),
        in_specs=[hbm] * (1 + len(tables)),
        out_specs=hbm,
        scratch_shapes=[
            pltpu.VMEM((PATHS * BLOCKS * ROWS, LANES), jnp.int32),
            *[pltpu.VMEM(table.shape, table.dtype) for table in tables],
            pltpu.VMEM((BATCH * OUT * PARTIAL, FOLD * LANES), jnp.bfloat16),
            pltpu.VMEM((PATHS * 2 * SLOT, LANES), jnp.float32),
            pltpu.VMEM((QUADS * PATHS, LANES), jnp.float32),
            pltpu.VMEM((QUADS * PATHS, LANES), jnp.bfloat16),
            pltpu.VMEM((times, rows, LANES), jnp.bfloat16),
            pltpu.VMEM((2, rows, LANES), jnp.bfloat16),
            dma((PATHS,)),
            dma((len(tables),)),
            dma((PIECES * (times - 1),)),
            dma((PIECES * (times - 1),)),
            dma,
            dma((PARTS,)),
            dma((PARTS,)),
            dma((PARTS,)),
        ],
        compiler_params=pltpu.CompilerParams(
            collective_id=0, has_side_effects=True, vmem_limit_bytes=60 * 2**20
        ),
        name="front",
    )(samples, *[jnp.asarray(table) for table in tables])


def run_correlate(slots, tile_map, spectra):
    return pl.pallas_call(
        functools.partial(correlate, slots),
        out_shape=jax.ShapeDtypeStruct((slots, CH_DEV, 2, TB, TB), jnp.float32),
        in_specs=[
            pl.BlockSpec(memory_space=pltpu.SMEM),
            pl.BlockSpec(memory_space=pltpu.VMEM),
        ],
        out_specs=pl.BlockSpec(memory_space=pl.ANY),
        scratch_shapes=[
            pltpu.VMEM((slots, CH_DEV, 2, TB, TB), jnp.float32),
            pltpu.SemaphoreType.DMA((slots,)),
        ],
        compiler_params=pltpu.CompilerParams(vmem_limit_bytes=40 * 2**20),
        name="correlate",
    )(tile_map, spectra)


def on_device(voltages, tile_map):
    freqs, times = lax.axis_size("freq"), lax.axis_size("tm")
    samples = voltages.reshape(PATHS, BLOCKS, 2, CHUNKS, LANES)
    samples = samples.transpose(0, 1, 3, 2, 4).reshape(PATHS * BLOCKS * ROWS, LANES)
    spectra = run_front(freqs, times, samples)
    return run_correlate(tile_map.shape[0] // times, tile_map, spectra)


def solution(mesh):
    in_specs = (P("freq", "tm", None, None), P())
    out_specs = P("tm", "freq", None, None, None)
    return jax.shard_map(
        on_device, mesh=mesh, in_specs=in_specs, out_specs=out_specs, check_vma=False
    )
```
